32 devices in a mesh: dp: 8 (over z, x), tensor: 4 (over y, core).
Axes of the slice: x: 2, y: 2, z: 4, core: 2. Of those that a mesh axis runs over, the one named last changes fastest.
Arguments:
- residual_in: bfloat16 [12288, 768], P(('dp', 'tensor')), may hold values from -6 to 6
- segments: int32 [8, 1536], P('dp'), may hold values from 0 to 3, as said below
- first_gain: float32 [768], replicated, may hold values from 0.5 to 1.5
- packed_weight: bfloat16 [768, 3, 768], P(None, None, 'tensor'), may hold values from -0.21875 to 0.21875
- output_weight: bfloat16 [768, 768], P('tensor'), may hold values from -6 to 6
- second_gain: float32 [768], replicated, may hold values from 0.5 to 1.5
- expand_weight: bfloat16 [768, 2, 1152], P(None, None, 'tensor'), may hold values from -0.21875 to 0.21875
- reduce_weight: bfloat16 [1152, 768], P('tensor'), may hold values from -0.1875 to 0.1875
- upstream: bfloat16 [12288, 768], P(('dp', 'tensor')), may hold values from -6 to 6
Outputs:
- residual_out: float32 [12288, 768], P(('dp', 'tensor'))
- input_back: float32 [12288, 768], P(('dp', 'tensor'))
- first_back: float32 [768], replicated
- packed_back: float32 [768, 3, 768], P(None, None, 'tensor')
- output_back: float32 [768, 768], P('tensor')
- second_back: float32 [768], replicated
- expand_back: float32 [768, 2, 1152], P(None, None, 'tensor')
- reduce_back: float32 [1152, 768], P('tensor')
The draws below stay inside these ranges and needn't reach their ends.
Inputs may be any that keep to these rules, and one draw needn't show every extreme that they name: `segments`: in every sequence the segment numbers never fall, begin at 0 and end at 3; segment 1 begins before position 384 and ends at or after position 1247.
All inputs are finite; a program needn't handle non-finite values.
Results may differ from the reference program's by a relative error of at most 0.015.
Values may be sent and summed in bfloat16 or wider, within the bound.
No kernel may reach another device: no remote copies, remote signals or barrier semaphores. Data moves between devices by JAX's collectives and lax.ppermute only.
A program may use at most 128 MiB of HBM per device.

```python
import math
import jax
import jax.numpy as jnp
from jax import lax

HEADS = 12
HEAD_DIM = 64
FF = 1152
LEN = 1536
D = 768
SEQS = 8
TOKENS = 12288


def segment_row(row_key):
    key_open, key_close, key_tail = jax.random.split(row_key, 3)
    opening = jax.random.randint(key_open, (), LEN // 16, LEN // 4)
    closing = jax.random.randint(key_close, (), LEN * 13 // 16, LEN * 15 // 16)
    tail_cut = jax.random.randint(key_tail, (), closing + 1, LEN)
    places = jnp.arange(LEN, dtype=jnp.int32)
    return (places >= opening).astype(jnp.int32) + (places >= closing).astype(jnp.int32) + (places >= tail_cut).astype(jnp.int32)


def draw_segments(key, part):
    key = jax.random.fold_in(key, 7)
    row_keys = jax.random.split(key, SEQS)
    return jax.vmap(segment_row)(row_keys)


def steps_of(stream_key, extent, cuts, smallest, largest):
    gain, own = 1.0, jax.random.fold_in(stream_key, 6)
    for dim, parts in cuts:
        heights = jnp.exp(jax.random.uniform(jax.random.fold_in(own, dim), (parts,), jnp.float32, smallest / len(cuts), largest / len(cuts)))
        gain = gain * jnp.repeat(heights, extent[dim] // parts).reshape([-1 if axis == dim else 1 for axis in range(len(extent))])
    return gain


def gaussian(key, extent, width, limit, pieces=(), kind=jnp.bfloat16):
    array = jax.random.normal(key, extent, jnp.float32) * width
    if len(pieces) > 0:
        array = steps_of(key, extent, pieces, -0.22, 0.18) * array
    return jnp.clip(array, min=-limit, max=limit).astype(kind)


def setup_inputs(seed: int = 0) -> dict:
    streams_of = jax.random.split(jax.random.key(seed), 10)
    return {
        "residual_in": gaussian(streams_of[0], (TOKENS, D), 1.0, 6.0, ((0, 32),)),
        "segments": draw_segments(jax.random.fold_in(streams_of[9], 71), 0),
        "first_gain": jnp.clip(1.0 + 0.1 * jax.random.normal(streams_of[2], (D,), jnp.float32), 0.5, 1.5),
        "packed_weight": gaussian(streams_of[3], (D, 3, D), D ** -0.5, 0.21875, ((2, 4),)),
        "output_weight": gaussian(streams_of[4], (D, D), (max(2 * D // LEN, 1)) ** -0.5, 6.0, ((0, 4),)),
        "second_gain": jnp.clip(1.0 + 0.1 * jax.random.normal(streams_of[5], (D,), jnp.float32), 0.5, 1.5),
        "expand_weight": gaussian(streams_of[6], (D, 2, FF), D ** -0.5, 0.21875, ((2, 4),)),
        "reduce_weight": gaussian(streams_of[7], (FF, D), FF ** -0.5, 0.1875, ((0, 4),)),
        "upstream": gaussian(streams_of[8], (TOKENS, D), 1.0, 6.0, ((0, 32),)),
    }


@jax.custom_vjp
def low(v):
    return lax.optimization_barrier(v.astype(jnp.bfloat16)).astype(jnp.float32)

@jax.custom_vjp
def low_back(v):
    return v

def low_keep(v):
    return (low(v), None)

def low_pass(kept, grad):
    return (grad,)

def back_keep(v):
    return (v, None)

def back_low(kept, grad):
    return (low(grad),)
low.defvjp(low_keep, low_pass)
low_back.defvjp(back_keep, back_low)
EPSILON = 1e-05
ROPE_BASE = 160000.0
SCALE = 0.125
MASKED = -1000000000.0
HIGH = lax.Precision.HIGHEST

def layer_norm(row_data, gain_vec):
    center = row_data - lax.optimization_barrier(jnp.mean(row_data, axis=-1, keepdims=True))
    spread = lax.optimization_barrier(jnp.mean(center * center, axis=-1, keepdims=True))
    return center * lax.rsqrt(spread + EPSILON) * gain_vec

def doc_positions(marks):
    step_index = jnp.arange(marks.shape[-1], dtype=jnp.int32)
    starts_here = jnp.concatenate([jnp.ones(marks.shape[:-1] + (1,), bool), marks[..., 1:] != marks[..., :-1]], axis=-1)
    begins = lax.cummax(jnp.where(starts_here, step_index, 0), axis=marks.ndim - 1)
    return step_index - begins

def rotary_tables(positions):
    half_index = jnp.arange(HEAD_DIM // 2, dtype=jnp.float32)
    inverse = jnp.exp(half_index * (-2.0 / HEAD_DIM) * math.log(ROPE_BASE))
    angles = positions.astype(jnp.float32)[:, None] * inverse[None, :]
    angles = jnp.concatenate([angles, angles], axis=-1)
    return (jnp.cos(angles), jnp.sin(angles))

def rotary(row_data, cosine, sine_tab):
    first_half = row_data[..., :HEAD_DIM // 2]
    second_half = row_data[..., HEAD_DIM // 2:]
    turned = jnp.concatenate([-second_half, first_half], axis=-1)
    return row_data * cosine[:, None, :] + turned * sine_tab[:, None, :]

def sequence_forward(row_data, seq_marks, gain_one, packed_mat, output_mat, gain_two, expand_mat, reduce_mat):
    normed = low(layer_norm(row_data, gain_one))
    packed = low_back(jnp.dot(normed, packed_mat.reshape(D, 3 * D), precision=HIGH))
    packed = packed.reshape(LEN, 3, HEADS, HEAD_DIM)
    cosine, sine_tab = rotary_tables(doc_positions(seq_marks))
    queries = low(rotary(packed[:, 0], cosine, sine_tab))
    key_rows = low(rotary(packed[:, 1], cosine, sine_tab))
    value_rows = low(packed[:, 2])
    same_doc = seq_marks[:, None] == seq_marks[None, :]

    def one_head(head_trio):
        head_query, head_key, head_value = head_trio
        scores = low_back(jnp.dot(head_query, head_key.T, precision=HIGH) * SCALE)
        scores = jnp.where(same_doc, scores, MASKED)
        row_top = lax.optimization_barrier(jnp.max(scores, axis=-1, keepdims=True))
        exponent = jnp.exp(scores - row_top)
        chance = low(exponent / lax.optimization_barrier(jnp.sum(exponent, axis=-1, keepdims=True)))
        return jnp.dot(chance, head_value, precision=HIGH)
    heads_out = lax.map(jax.checkpoint(one_head), (queries.transpose(1, 0, 2), key_rows.transpose(1, 0, 2), value_rows.transpose(1, 0, 2)))
    attended = low_back(low(heads_out.transpose(1, 0, 2).reshape(LEN, D)))
    middle = row_data + low_back(jnp.dot(attended, output_mat, precision=HIGH))
    normed_two = low(layer_norm(middle, gain_two))
    gate_up = low_back(jnp.dot(normed_two, expand_mat.reshape(D, 2 * FF), precision=HIGH)).reshape(LEN, 2, FF)
    hidden = low(jax.nn.gelu(gate_up[:, 0], approximate=False) * gate_up[:, 1])
    return middle + low_back(jnp.dot(hidden, reduce_mat, precision=HIGH))

def reference(residual_in, segments, first_gain, packed_weight, output_weight, second_gain, expand_weight, reduce_weight, upstream):
    weights = (first_gain.astype(jnp.float32), packed_weight.astype(jnp.float32), output_weight.astype(jnp.float32), second_gain.astype(jnp.float32), expand_weight.astype(jnp.float32), reduce_weight.astype(jnp.float32))
    row_blocks = residual_in.astype(jnp.float32).reshape(SEQS, LEN, D)
    slope_blocks = upstream.astype(jnp.float32).reshape(SEQS, LEN, D)

    def seq_step(totals, seq_item):
        row_data, seq_marks, slope_rows = seq_item

        def forward(row_vals, gain_one, packed_mat, output_mat, gain_two, expand_mat, reduce_mat):
            return sequence_forward(row_vals, seq_marks, gain_one, packed_mat, output_mat, gain_two, expand_mat, reduce_mat)
        result, pullback = jax.vjp(forward, row_data, weights[0], weights[1], weights[2], weights[3], weights[4], weights[5])
        gradient = pullback(slope_rows)
        return (jax.tree.map(jnp.add, totals, tuple(gradient[1:])), (result, gradient[0]))
    zero_sums = jax.tree.map(jnp.zeros_like, weights)
    weight_totals, (outputs_seq, inputs_back) = lax.scan(seq_step, zero_sums, (row_blocks, segments, slope_blocks))
    return (outputs_seq.reshape(TOKENS, D), inputs_back.reshape(TOKENS, D), weight_totals[0], weight_totals[1], weight_totals[2], weight_totals[3], weight_totals[4], weight_totals[5])
```

```python
from functools import partial
import math

import jax
import jax.numpy as jnp
from jax import lax
from jax.experimental import pallas as pl
from jax.experimental.pallas import tpu as pltpu
from jax.sharding import PartitionSpec as P

HEAD_DIM = 64
LANES = 128
EPSILON = 1e-05
ROPE_BASE = 160000.0
SCALE = 0.125
MASKED = -1000000000.0
MARK_LANE = 64
ONES_LANE = 68
TOTAL_LANE = 64

F32 = jnp.float32
LOW = jnp.bfloat16
NT = (((1,), (1,)), ((), ()))
TN = (((0,), (0,)), ((), ()))


def swap(value, offset):
    size = lax.axis_size("tensor")
    return lax.ppermute(value, "tensor", [(i, i ^ offset) for i in range(size)])


def gather_blocks(own):
    from_chip = swap(own, 2)
    from_core = swap(own, 1)
    return [own, from_core, from_chip, swap(from_chip, 1)]


def exchange_blocks(blocks):
    return [blocks[0]] + [swap(blocks[j], j) for j in (1, 2, 3)]


def scatter_blocks(blocks):
    near = [blocks[0].astype(F32) + swap(blocks[1].astype(LOW), 1).astype(F32)]
    near.append(blocks[2].astype(F32) + swap(blocks[3].astype(LOW), 1).astype(F32))
    return near[0] + swap(near[1].astype(LOW), 2).astype(F32)


def dp_stages(size):
    stages, step = [], 1
    while step < size:
        group = 2 if step == 1 or size // step == 2 else 4
        stages.append((step, group))
        step *= group
    return stages


def dp_swap(value, offset):
    size = lax.axis_size("dp")
    return lax.ppermute(value, "dp", [(i, i ^ offset) for i in range(size)])


def gain_rows(gains):
    return jnp.concatenate(list(split_three(gains)) + [jnp.zeros_like(gains, LOW)])


def gain_sum(gains, rows):
    return gains + (rows[0:2].astype(F32) + rows[2:4].astype(F32) + rows[4:6].astype(F32))


def dp_sum(value, gains=None):
    me = lax.axis_index("dp")
    stages = dp_stages(lax.axis_size("dp"))
    value = value.astype(LOW)
    half = value.shape[1] // 2
    odd = me % 2 == 1
    left, right = value[:, :half], value[:, half:]
    got = dp_swap(jnp.where(odd, left, right), 1)
    value = (jnp.where(odd, right, left).astype(F32) + got.astype(F32)).astype(LOW)
    for step, group in stages[1:]:
        mine = (me // step) % group
        rows = value.shape[0] // group
        pick = lambda k: lax.dynamic_slice_in_dim(value, (mine ^ k) * rows, rows, 0)
        total = pick(0).astype(F32)
        old = gains
        for k in range(1, group):
            if gains is None:
                got = dp_swap(pick(k), k * step)
            else:
                got = dp_swap(jnp.concatenate([pick(k)] + halves(gain_rows(old))), k * step)
                gains = gain_sum(gains, join_halves(got[rows:], 8))
            total = total + got[:rows].astype(F32)
        value = total.astype(LOW)
    for step, group in stages[:0:-1]:
        mine = (me // step) % group
        parts = jnp.stack([value] + [dp_swap(value, k * step) for k in range(1, group)])
        value = jnp.concatenate(
            [lax.dynamic_index_in_dim(parts, mine ^ k, 0, keepdims=False) for k in range(group)]
        )
    if gains is None:
        got = dp_swap(value, 1)
    else:
        rows = value.shape[0]
        got = dp_swap(jnp.concatenate([value] + halves(gain_rows(gains))), 1)
        gains = gain_sum(gains, join_halves(got[rows:], 8))
        got = got[:rows]
    value = jnp.concatenate([jnp.where(odd, got, value), jnp.where(odd, value, got)], axis=1).astype(F32)
    return value if gains is None else (value, gains)


def halves(rows):
    half = rows.shape[1] // 2
    return [rows[:, :half], rows[:, half:]]


def join_halves(rows, count):
    return jnp.concatenate([rows[:count], rows[count : 2 * count]], axis=1)


def layer_norm(row_data, gain_vec):
    center = row_data - jnp.mean(row_data, axis=-1, keepdims=True)
    spread = jnp.mean(center * center, axis=-1, keepdims=True)
    return center * lax.rsqrt(spread + EPSILON) * gain_vec


def doc_positions(marks):
    step_index = jnp.arange(marks.shape[-1], dtype=jnp.int32)
    starts_here = jnp.concatenate([jnp.ones((1,), bool), marks[1:] != marks[:-1]], axis=-1)
    begins = lax.cummax(jnp.where(starts_here, step_index, 0), axis=0)
    return step_index - begins


def rotary_tables(positions):
    half_index = jnp.arange(HEAD_DIM // 2, dtype=F32)
    inverse = jnp.exp(half_index * (-2.0 / HEAD_DIM) * math.log(ROPE_BASE))
    angles = positions.astype(F32)[:, None] * inverse[None, :]
    angles = jnp.concatenate([angles, angles], axis=-1)
    return (jnp.cos(angles), jnp.sin(angles))


def turn(row_data):
    half = HEAD_DIM // 2
    return jnp.concatenate([-row_data[..., half:], row_data[..., :half]], axis=-1)


def split_three(value):
    high = value.astype(LOW)
    rest = value - high.astype(F32)
    middle = rest.astype(LOW)
    return high, middle, (rest - middle.astype(F32)).astype(LOW)


def put_three(base, first, column):
    lane = lax.broadcasted_iota(jnp.int32, base.shape, 1)
    out = base.astype(F32)
    for step, part in enumerate(split_three(column)):
        out = jnp.where(lane == first + step, part.astype(F32), out)
    return out.astype(LOW)


def forward_kernel(query_ref, key_ref, value_ref, out_ref, widened_ref):
    query = query_ref[0]
    scores = lax.dot_general(query, key_ref[0], NT, preferred_element_type=F32)
    top = jnp.max(scores, axis=1, keepdims=True)
    exponent = jnp.exp(scores - top).astype(LOW)
    out = jnp.dot(exponent, value_ref[0], preferred_element_type=F32)
    totals = out[:, TOTAL_LANE : TOTAL_LANE + 1]
    out_ref[0] = (out / totals).astype(LOW)
    widened_ref[0] = put_three(query, ONES_LANE, -(top + jnp.log(totals)))


def attend_forward(queries, keys, values):
    heads, rows, _ = queries.shape
    block = 512
    row_spec = pl.BlockSpec((1, block, LANES), lambda h, i: (h, i, 0))
    all_spec = pl.BlockSpec((1, rows, LANES), lambda h, i: (h, 0, 0))
    return pl.pallas_call(
        forward_kernel,
        grid=(heads, rows // block),
        in_specs=[row_spec, all_spec, all_spec],
        out_specs=[row_spec, row_spec],
        out_shape=[jax.ShapeDtypeStruct((heads, rows, LANES), LOW)] * 2,
        compiler_params=pltpu.CompilerParams(vmem_limit_bytes=40 * 2**20),
        cost_estimate=pl.CostEstimate(
            flops=16 * heads * rows * rows * HEAD_DIM,
            bytes_accessed=10 * heads * rows * LANES,
            transcendentals=heads * rows * rows,
        ),
        name="attend_forward",
    )(queries, keys, values)


def backward_kernel(chunk, query_ref, key_ref, value_ref, out_ref, slope_ref, dq_ref, dk_ref, dv_ref, total_ref):
    slope = slope_ref[0]
    centre = jnp.sum(slope.astype(F32) * out_ref[0].astype(F32), axis=1, keepdims=True)
    widened = put_three(slope, TOTAL_LANE, -centre)
    query = query_ref[0]
    rows = key_ref.shape[1]

    @pl.when(pl.program_id(1) == 0)
    def _():
        dk_ref[...] = jnp.zeros_like(dk_ref)
        dv_ref[...] = jnp.zeros_like(dv_ref)

    total_ref[...] = jnp.zeros_like(total_ref)
    for first in range(0, rows, chunk):
        here = pl.ds(first, chunk)
        keys = key_ref[0, here, :]
        chance = jnp.exp(lax.dot_general(keys, query, NT, preferred_element_type=F32))
        drift = lax.dot_general(value_ref[0, here, :], widened, NT, preferred_element_type=F32)
        score_slope = (chance * drift).astype(LOW)
        dv_ref[0, here, :] += jnp.dot(chance.astype(LOW), slope, preferred_element_type=F32)
        dk_ref[0, here, :] += jnp.dot(score_slope, query, preferred_element_type=F32)
        total_ref[...] += lax.dot_general(score_slope, keys, TN, preferred_element_type=F32)
    dq_ref[0] = total_ref[...] * SCALE


def attend_backward(widened, keys, values, attended, slopes):
    heads, rows, _ = keys.shape
    block, chunk = 512, 512
    row_spec = pl.BlockSpec((1, block, LANES), lambda h, i: (h, i, 0))
    all_spec = pl.BlockSpec((1, rows, LANES), lambda h, i: (h, 0, 0))
    return pl.pallas_call(
        partial(backward_kernel, chunk),
        grid=(heads, rows // block),
        in_specs=[row_spec, all_spec, all_spec, row_spec, row_spec],
        out_specs=[row_spec, all_spec, all_spec],
        out_shape=[jax.ShapeDtypeStruct((heads, rows, LANES), F32)] * 3,
        scratch_shapes=[pltpu.VMEM((block, LANES), F32)],
        compiler_params=pltpu.CompilerParams(vmem_limit_bytes=40 * 2**20),
        cost_estimate=pl.CostEstimate(
            flops=40 * heads * rows * rows * HEAD_DIM,
            bytes_accessed=20 * heads * rows * LANES,
            transcendentals=heads * rows * rows,
        ),
        name="attend_backward",
    )(widened, keys, values, attended, slopes)


def outer_sum(left, right):
    return lax.dot_general(left, right, TN, preferred_element_type=F32)


def against(left, right):
    return lax.dot_general(left, right, NT, preferred_element_type=F32)


def norm_pull(slope, row_data, gain_vec):
    center = row_data - jnp.mean(row_data, axis=-1, keepdims=True)
    scale = lax.rsqrt(jnp.mean(center * center, axis=-1, keepdims=True) + EPSILON)
    normal = center * scale
    inner = slope * gain_vec
    pulled = scale * (
        inner
        - jnp.mean(inner, axis=-1, keepdims=True)
        - normal * jnp.mean(inner * normal, axis=-1, keepdims=True)
    )
    return pulled, jnp.sum(slope * normal, axis=0)


def widen(row_heads, extra):
    upper = jnp.broadcast_to(extra[:, None, :], row_heads.shape)
    return jnp.concatenate([row_heads, upper], axis=-1).transpose(1, 0, 2).astype(LOW)


def per_device(
    residual_in,
    segments,
    first_gain,
    packed_weight,
    output_weight,
    second_gain,
    expand_weight,
    reduce_weight,
    upstream,
):
    rows_local, width = residual_in.shape
    me = lax.axis_index("tensor")
    heads = packed_weight.shape[2] // HEAD_DIM
    units = expand_weight.shape[2]
    row_data = residual_in.astype(F32)
    normed_blocks = gather_blocks(layer_norm(row_data, first_gain).astype(LOW))
    packed_flat = packed_weight.reshape(width, -1)
    output_all = jnp.concatenate(gather_blocks(output_weight))
    expand_all = jnp.concatenate(gather_blocks(expand_weight.reshape(width, -1)), axis=1)
    reduce_all = jnp.concatenate(gather_blocks(reduce_weight))

    marks = segments[0]
    cosine, sine = rotary_tables(doc_positions(marks))
    by_block = lambda table: jnp.concatenate(
        [lax.dynamic_slice_in_dim(table, (me ^ j) * rows_local, rows_local, 0) for j in range(4)]
    )
    marks, cosine, sine = by_block(marks), by_block(cosine), by_block(sine)
    same = (marks[:, None] == jnp.arange(4)[None, :]).astype(F32)
    total_rows = marks.shape[0]
    blank = jnp.zeros((total_rows, 60), F32)
    ones = jnp.ones((total_rows, 3), F32)
    query_extra = jnp.concatenate([MASKED * (1.0 - same), blank], axis=1)
    key_extra = jnp.concatenate([same, ones, blank[:, 3:]], axis=1)
    value_extra = jnp.concatenate([ones, blank, blank[:, :1]], axis=1)

    normed_all = jnp.concatenate(normed_blocks)
    packed_raw = jnp.dot(normed_all, packed_flat, preferred_element_type=F32)
    packed_raw = packed_raw.reshape(total_rows, 3, heads, HEAD_DIM)
    rope = lambda v: v * cosine[:, None, :] + turn(v) * sine[:, None, :]
    queries = widen(rope(packed_raw[:, 0]) * SCALE, query_extra)
    keys = widen(rope(packed_raw[:, 1]), key_extra)
    values = widen(packed_raw[:, 2], value_extra)
    attended, widened = attend_forward(queries, keys, values)
    flat = attended[:, :, :HEAD_DIM].transpose(1, 0, 2).reshape(4, rows_local, heads * HEAD_DIM)
    mine = jnp.concatenate(exchange_blocks([flat[j] for j in range(4)]), axis=1)

    middle = row_data + jnp.dot(mine, output_all, preferred_element_type=F32)
    normed_two = layer_norm(middle, second_gain).astype(LOW)
    gate_up = jnp.dot(normed_two, expand_all, preferred_element_type=F32)
    gate_up = gate_up.reshape(rows_local, 4, 2, units)
    gate, up = gate_up[:, :, 0].reshape(rows_local, -1), gate_up[:, :, 1].reshape(rows_local, -1)
    bell = 0.5 * (1.0 + lax.erf(gate * math.sqrt(0.5)))
    active = gate * bell
    hidden = (active * up).astype(LOW)
    residual_out = middle + jnp.dot(hidden, reduce_all, preferred_element_type=F32)
    hidden_slope = against(upstream, reduce_all)
    bell_slope = bell + gate * jnp.exp(-0.5 * gate * gate) * (1.0 / math.sqrt(2.0 * math.pi))
    gate_slope = (hidden_slope * up * bell_slope).reshape(rows_local, 4, 1, units)
    up_slope = (hidden_slope * active).reshape(rows_local, 4, 1, units)
    gate_up_slope = jnp.concatenate([gate_slope, up_slope], axis=2).astype(LOW).reshape(rows_local, -1)
    middle_part, second_part = norm_pull(against(gate_up_slope, expand_all), middle, second_gain)
    middle_slope = upstream.astype(F32) + middle_part
    middle_low = middle_slope.astype(LOW)
    attended_slope = against(middle_low, output_all).astype(LOW).reshape(rows_local, 4, -1)
    slopes = jnp.concatenate(exchange_blocks([attended_slope[:, j] for j in range(4)]))
    slopes = widen(slopes.reshape(total_rows, heads, HEAD_DIM), jnp.zeros((total_rows, HEAD_DIM), LOW))

    reduce_part = outer_sum(hidden, upstream).reshape(4, units, width)
    expand_part = outer_sum(gate_up_slope, normed_two).reshape(4, 2 * units, width)
    output_part = outer_sum(mine, middle_low).reshape(4, -1, width)
    owned = [
        scatter_blocks([part[j] for j in range(4)]) for part in (reduce_part, expand_part, output_part)
    ]
    owned = dp_sum(jnp.concatenate(owned))
    reduce_back, expand_back, output_back = owned[:units], owned[units : 3 * units], owned[3 * units :]

    dq, dk, dv = attend_backward(widened, keys, values, attended, slopes)
    rope_pull = lambda v: v * cosine[None] - turn(v) * sine[None]
    packed_slope = jnp.stack(
        [rope_pull(dq[..., :HEAD_DIM]), rope_pull(dk[..., :HEAD_DIM]), dv[..., :HEAD_DIM]]
    )
    packed_slope = packed_slope.astype(LOW).transpose(2, 0, 1, 3).reshape(total_rows, -1)
    packed_part = outer_sum(packed_slope, normed_all)
    normed_slope = against(packed_slope, packed_flat).reshape(4, rows_local, width)
    normed_slope = scatter_blocks([normed_slope[j] for j in range(4)])
    first_part = jnp.sum(packed_part * packed_flat.T.astype(F32), axis=0) / first_gain
    gains = jnp.stack([first_part, second_part])
    gains = sum([swap(gains, j) for j in (1, 2, 3)], gains)
    packed_back, gains = dp_sum(packed_part, gains)
    input_part = norm_pull(normed_slope, row_data, first_gain)[0]
    input_back = middle_slope + input_part
    first_back, second_back = gains[0], gains[1]
    return (
        residual_out,
        input_back,
        first_back,
        packed_back.T.reshape(width, 3, -1),
        output_back,
        second_back,
        expand_back.T.reshape(width, 2, units),
        reduce_back,
    )


def solution(mesh):
    rows = P(("dp", "tensor"), None)
    placed = (
        rows,
        P("dp", None),
        P(),
        P(None, None, "tensor"),
        P("tensor", None),
        P(),
        P(None, None, "tensor"),
        P("tensor", None),
        rows,
    )
    return jax.shard_map(
        per_device,
        mesh=mesh,
        in_specs=placed,
        out_specs=(rows, rows, P(), placed[3], placed[4], P(), placed[6], placed[7]),
        check_vma=False,
    )
```

```python
from functools import partial
import math

import jax
import jax.numpy as jnp
from jax import lax
from jax.experimental import pallas as pl
from jax.experimental.pallas import tpu as pltpu
from jax.sharding import PartitionSpec as P

HEAD_DIM = 64
LANES = 128
EPSILON = 1e-05
ROPE_BASE = 160000.0
SCALE = 0.125
MASKED = -1000000000.0
MARKS = 4
MARK_LANE = 64
LOG_LANE = 68
SUM_LANE = 64
VMEM_BYTES = 48 * 2**20

F32 = jnp.float32
LOW = jnp.bfloat16
NT = (((1,), (1,)), ((), ()))
TN = (((0,), (0,)), ((), ()))


def dot(left, right):
    return jnp.dot(left, right, preferred_element_type=F32)


def against(left, right):
    return lax.dot_general(left, right, NT, preferred_element_type=F32)


def outer_sum(left, right):
    return lax.dot_general(left, right, TN, preferred_element_type=F32)


def call(kernel, out_shapes, args, flops, name, **rest):
    shapes = [jax.ShapeDtypeStruct(shape, kind) for shape, kind in out_shapes]
    moved = sum(a.size * a.dtype.itemsize for a in list(args) + shapes)
    return pl.pallas_call(
        kernel,
        out_shape=shapes,
        compiler_params=pltpu.CompilerParams(vmem_limit_bytes=VMEM_BYTES),
        cost_estimate=pl.CostEstimate(flops=int(flops), bytes_accessed=int(moved), transcendentals=0),
        name=name,
        **rest,
    )(*args)


def lane_of(shape):
    return lax.broadcasted_iota(jnp.int32, shape, 1)


def split_three(value):
    high = value.astype(LOW)
    rest = value - high.astype(F32)
    middle = rest.astype(LOW)
    return high, middle, (rest - middle.astype(F32)).astype(LOW)


def put_three(base, first, column):
    lane = lane_of(base.shape)
    out = base.astype(F32)
    for step, part in enumerate(split_three(column)):
        out = jnp.where(lane == first + step, part.astype(F32), out)
    return out.astype(LOW)


def head_lanes(head, heads):
    shape = (heads * HEAD_DIM, LANES)
    source = lax.broadcasted_iota(jnp.int32, shape, 0)
    lane = lane_of(shape)
    return jnp.where((lane < HEAD_DIM) & (source == lane + head * HEAD_DIM), 1.0, 0.0).astype(LOW)


def turn_lanes(rows):
    lane = lane_of(rows.shape)
    first = lane % HEAD_DIM < HEAD_DIM // 2
    return jnp.where(first, pltpu.roll(rows, LANES - HEAD_DIM // 2, 1), pltpu.roll(rows, HEAD_DIM // 2, 1))


def packed_lanes(parts):
    keep = lane_of(parts[0].shape) < HEAD_DIM
    tiles = []
    for i in range(0, len(parts), 2):
        left = parts[i].astype(F32)
        right = pltpu.roll(parts[i + 1].astype(F32), HEAD_DIM, 1) if i + 1 < len(parts) else 0.0
        tiles.append(jnp.where(keep, left, right).astype(LOW))
    return jnp.concatenate(tiles, axis=1)


def project_kernel(heads, *refs):
    normed_refs, (weight_ref, cos_ref, sin_ref, mark_ref, query_ref, key_ref, value_ref) = refs[:2], refs[2:]
    for b, normed_ref in enumerate(normed_refs):
        rows = normed_ref.shape[0]
        here = pl.ds(b * rows, rows)
        packed = against(normed_ref[...], weight_ref[...])
        cosine, sine = cos_ref[here, :], sin_ref[here, :]
        lane = lane_of(cosine.shape)
        upper = lane - MARK_LANE
        same = upper == mark_ref[here, :]
        marks = (upper >= 0) & (upper < MARKS)
        logs = (lane >= LOG_LANE) & (lane < LOG_LANE + 3)
        sums = (lane >= SUM_LANE) & (lane < SUM_LANE + 3)
        extras = (
            jnp.where(marks & jnp.logical_not(same), MASKED, 0.0),
            jnp.where((marks & same) | logs, 1.0, 0.0),
            jnp.where(sums, 1.0, 0.0),
        )
        tiles = [packed[:, i : i + LANES] for i in range(0, packed.shape[1], LANES)]
        for i in range(3 * heads):
            rows_part = tiles[i // 2]
            part, head = i // heads, i % heads
            if part < 2:
                rows_part = rows_part * cosine + turn_lanes(rows_part) * sine
            if i % 2 == 1:
                rows_part = pltpu.roll(rows_part, HEAD_DIM, 1)
            if part == 0:
                rows_part = rows_part * SCALE
            out_ref = (query_ref, key_ref, value_ref)[part]
            out_ref[head, here, :] = jnp.where(lane < HEAD_DIM, rows_part, extras[part]).astype(LOW)


def project(normed, weight, cosine, sine, marks, heads):
    rows, width = normed[0].shape
    return call(
        partial(project_kernel, heads),
        [((heads, 2 * rows, LANES), LOW)] * 3,
        (*normed, weight, cosine, sine, marks),
        4 * rows * width * weight.shape[0],
        "project",
    )


def forward_kernel(query_ref, near_key, far_key, near_value, far_value, out_a, out_b, widened_ref):
    heads, half, _ = query_ref.shape
    outs = {0: out_a, half // 2: out_b}
    jobs = [(head, first) for first in outs for head in range(heads)]

    def scores(head, first):
        query = query_ref[head, pl.ds(first, half // 2), :]
        return query, against(query, near_key[head]), against(query, far_key[head])

    following = scores(*jobs[0])
    for i, (head, first) in enumerate(jobs):
        query, near, far = following
        if i + 1 < len(jobs):
            following = scores(*jobs[i + 1])
        top = jnp.maximum(jnp.max(near, axis=1, keepdims=True), jnp.max(far, axis=1, keepdims=True))
        out = dot(jnp.exp(near - top).astype(LOW), near_value[head])
        out = out + dot(jnp.exp(far - top).astype(LOW), far_value[head])
        sums = out[:, SUM_LANE : SUM_LANE + 1]
        widened_ref[head, pl.ds(first, half // 2), :] = put_three(query, LOG_LANE, -(top + jnp.log(sums)))
        part = against((out / sums).astype(LOW), head_lanes(head, heads))
        total = part if head == 0 else total + part
        if head == heads - 1:
            outs[first][...] = total.astype(LOW)


def attend_forward(queries, near, far):
    heads, half, _ = queries.shape
    return call(
        forward_kernel,
        [((half // 2, heads * HEAD_DIM), LOW)] * 2 + [(queries.shape, LOW)],
        (queries, near[0], far[0], near[1], far[1]),
        32 * heads * half * half * HEAD_DIM,
        "attend_forward",
    )


def backward_kernel(heads, chunk, last, *refs):
    query_ref, near_key, far_key, near_value, far_value, out_a, out_b, slope_a, slope_b = refs[:9]
    cos_ref, sin_ref = refs[9:11]
    if last:
        key_start, value_start, cos_all, sin_all = refs[11:15]
    dq_ref, dk_ref, dv_ref = refs[-3:]
    half = query_ref.shape[1]
    pick = head_lanes(pl.program_id(0), heads)
    slope = dot(jnp.concatenate([slope_a[...], slope_b[...]]), pick)
    centre = jnp.sum(slope * dot(jnp.concatenate([out_a[...], out_b[...]]), pick), axis=1, keepdims=True)
    slope = slope.astype(LOW)
    widened = put_three(slope, SUM_LANE, -centre)
    query = query_ref[0]
    keep = lane_of((chunk, LANES)) < HEAD_DIM
    sides = ((near_key, near_value), (far_key, far_value))
    jobs = [(side, first) for side in (0, 1) for first in range(0, half, chunk)]

    def scores(side, first):
        keys = sides[side][0][0, pl.ds(first, chunk), :]
        values = sides[side][1][0, pl.ds(first, chunk), :]
        return keys, against(keys, query), against(values, widened)

    following = scores(*jobs[0])
    total = None
    for i, (side, first) in enumerate(jobs):
        keys, chance, drift = following
        if i + 1 < len(jobs):
            following = scores(*jobs[i + 1])
        here = pl.ds(side * half + first, chunk)
        chance = jnp.exp(chance)
        score_slope = (chance * drift).astype(LOW)
        dv = dot(chance.astype(LOW), slope)
        dk = dot(score_slope, query)
        if last:
            dk = dk + key_start[0, here, :]
            dk = dk * cos_all[here, :] - turn_lanes(dk) * sin_all[here, :]
            dk = jnp.where(keep, dk, 0.0).astype(LOW)
            dv = jnp.where(keep, dv + value_start[0, here, :], 0.0).astype(LOW)
        dk_ref[0, here, :] = dk
        dv_ref[0, here, :] = dv
        part = outer_sum(score_slope, keys)
        total = part if total is None else total + part
    total = total * SCALE
    total = total * cos_ref[...] - turn_lanes(total) * sin_ref[...]
    dq_ref[0] = jnp.where(lane_of(total.shape) < HEAD_DIM, total, 0.0).astype(LOW)


def attend_backward(widened, near, far, outs, slopes, tables, started=None, all_tables=None):
    heads, half, _ = widened.shape
    head = pl.BlockSpec((1, half, LANES), lambda h: (h, 0, 0))
    long = pl.BlockSpec((1, 2 * half, LANES), lambda h: (h, 0, 0))
    flat = pl.BlockSpec(outs[0].shape, lambda h: (0, 0))
    table = pl.BlockSpec((half, LANES), lambda h: (0, 0))
    long_table = pl.BlockSpec((2 * half, LANES), lambda h: (0, 0))
    args = (widened, near[0], far[0], near[1], far[1], *outs, *slopes, *tables)
    specs = [head] * 5 + [flat] * 4 + [table] * 2
    last = started is not None
    if last:
        args += (*started, *all_tables)
        specs += [long] * 2 + [long_table] * 2
    full = (heads, 2 * half, LANES)
    kind = LOW if last else F32
    return call(
        partial(backward_kernel, heads, half, last),
        [(widened.shape, LOW), (full, kind), (full, kind)],
        args,
        80 * heads * half * half * HEAD_DIM,
        "attend_backward",
        grid=(heads,),
        in_specs=specs,
        out_specs=[head, long, long],
    )


def mean_of(rows):
    return jnp.mean(rows, axis=-1, keepdims=True)


def normal_of(rows):
    center = rows - mean_of(rows)
    scale = lax.rsqrt(mean_of(center * center) + EPSILON)
    return center * scale, scale


def norm_pull(slope, normal, scale, gain):
    inner = slope * gain
    return scale * (inner - mean_of(inner) - normal * mean_of(inner * normal))


def middle_kernel(*refs):
    attended, weights, (rows_ref, gain_ref, middle_ref, normed_ref) = refs[:4], refs[4:8], refs[8:]
    middle = rows_ref[...].astype(F32)
    for attended_ref, weight_ref in zip(attended, weights):
        middle = middle + dot(attended_ref[...], weight_ref[...])
    middle_ref[...] = middle
    normed_ref[...] = (normal_of(middle)[0] * gain_ref[...]).astype(LOW)


def gelu_parts(gate):
    bell = 0.5 * (1.0 + lax.erf(gate * math.sqrt(0.5)))
    slope = bell + gate * jnp.exp(-0.5 * gate * gate) * (1.0 / math.sqrt(2.0 * math.pi))
    return gate * bell, slope


def unit_slopes(normed, slope_rows, expand_ref, reduce_ref):
    units = reduce_ref.shape[0]
    active, active_slope = gelu_parts(against(normed, expand_ref[:units, :]))
    up = against(normed, expand_ref[units:, :])
    hidden_slope = against(slope_rows, reduce_ref[...])
    hidden = (active * up).astype(LOW)
    return hidden, (hidden_slope * up * active_slope).astype(LOW), (hidden_slope * active).astype(LOW)


def feed_kernel(*refs):
    expand, reduce, output = refs[:4], refs[4:8], refs[8:12]
    middle_ref, normed_ref, upstream_ref, gain_ref = refs[12:16]
    out_ref, slope_ref, low_ref, gain_sum_ref = refs[16:20]
    attended_slopes = refs[20:]
    middle, upstream = middle_ref[...], upstream_ref[...]
    out, normed_slope = middle, None
    for expand_ref, reduce_ref in zip(expand, reduce):
        units = reduce_ref.shape[0]
        hidden, gate_slope, up_slope = unit_slopes(normed_ref[...], upstream, expand_ref, reduce_ref)
        out = out + dot(hidden, reduce_ref[...])
        part = dot(gate_slope, expand_ref[:units, :]) + dot(up_slope, expand_ref[units:, :])
        normed_slope = part if normed_slope is None else normed_slope + part
    out_ref[...] = out
    normal, scale = normal_of(middle)
    gain_sum_ref[...] = jnp.sum(normed_slope * normal, axis=0, keepdims=True)
    slope = upstream.astype(F32) + norm_pull(normed_slope, normal, scale, gain_ref[...])
    slope_ref[...] = slope
    low = slope.astype(LOW)
    low_ref[...] = low
    for weight_ref, attended_slope_ref in zip(output, attended_slopes):
        attended_slope_ref[...] = against(low, weight_ref[...]).astype(LOW)


def output_sums_kernel(*refs):
    attended, low_ref, outs = refs[:4], refs[4], refs[5:]
    for attended_ref, out_ref in zip(attended, outs):
        out_ref[...] = outer_sum(attended_ref[...], low_ref[...]).astype(LOW)


def unit_sums_kernel(*refs):
    normed, upstream, (expand_ref, reduce_ref, out_ref, total_ref) = refs[:4], refs[4:8], refs[8:]
    units = reduce_ref.shape[0]
    for b, (normed_ref, upstream_ref) in enumerate(zip(normed, upstream)):
        parts = unit_slopes(normed_ref[...], upstream_ref[...], expand_ref, reduce_ref)
        for i, (part, other_ref) in enumerate(zip(parts, (upstream_ref, normed_ref, normed_ref))):
            here = pl.ds(i * units, units)
            total = outer_sum(part, other_ref[...])
            total_ref[here, :] = total if b == 0 else total_ref[here, :] + total
    out_ref[...] = total_ref[...].astype(LOW)


def packed_sums_kernel(heads, *refs):
    dq_a, dq_b, dk, dv, normed, (weight_ref, gain_ref) = *refs[:4], refs[4:8], refs[8:10]
    out_ref, gain_sum_ref, slope_refs, total_ref = refs[10], refs[11], refs[12:16], refs[16]
    rows = normed[0].shape[0]
    used = out_ref.shape[0]
    for b in range(4):
        here = pl.ds(b * rows, rows)
        dq = dq_a if b < 2 else dq_b
        parts = [dq[h, pl.ds((b % 2) * rows, rows), :] for h in range(heads)]
        parts += [ref[h, here, :] for ref in (dk, dv) for h in range(heads)]
        slope = packed_lanes(parts)
        slope_refs[b][...] = slope
        total = outer_sum(slope, normed[b][...])
        total_ref[...] = total if b == 0 else total_ref[...] + total
    total = total_ref[:used, :]
    out_ref[...] = total.astype(LOW)
    weight = weight_ref[:used, :].astype(F32)
    gain_sum_ref[...] = jnp.sum(total * weight, axis=0, keepdims=True) / gain_ref[...]


def normed_slope_kernel(*refs):
    slopes, weight_ref, outs = refs[:4], refs[4], refs[5:]
    for slope_ref, out_ref in zip(slopes, outs):
        out_ref[...] = dot(slope_ref[...], weight_ref[...]).astype(out_ref.dtype)


def swap(value, offset):
    size = lax.axis_size("tensor")
    return lax.ppermute(value, "tensor", [(i, i ^ offset) for i in range(size)])


def dp_swap(value, offset):
    size = lax.axis_size("dp")
    return lax.ppermute(value, "dp", [(i, i ^ offset) for i in range(size)])


def gather_blocks(own):
    from_core = swap(own, 1)
    from_chip = swap(own, 2)
    return [own, from_core, from_chip, swap(from_chip, 1)]


def scatter_blocks(blocks):
    near = blocks[0].astype(F32) + swap(blocks[1], 1).astype(F32)
    far = blocks[2].astype(F32) + swap(blocks[3], 1).astype(F32)
    return near + swap(far.astype(LOW), 2).astype(F32)


def add_low(left, right):
    return (left.astype(F32) + right.astype(F32)).astype(LOW)


def cut(value, odd, axis):
    half = value.shape[axis] // 2
    lower, upper = (lax.slice_in_dim(value, i * half, (i + 1) * half, axis=axis) for i in range(2))
    return jnp.where(odd, upper, lower), jnp.where(odd, lower, upper)


def join(value, got, odd, axis):
    return jnp.concatenate([jnp.where(odd, got, value), jnp.where(odd, value, got)], axis=axis)


def gain_rows(gains, columns):
    rows = jnp.concatenate(split_three(gains)).reshape(-1, columns)
    return jnp.pad(rows, ((0, -rows.shape[0] % 16), (0, 0)))


def gain_sum(gains, rows):
    parts = rows[: 3 * gains.size // rows.shape[1]].reshape((3,) + gains.shape).astype(F32)
    return gains + parts[0] + parts[1] + parts[2]


def dp_sum(value, order, gains=None):
    me = lax.axis_index("dp")
    summed = gains
    for i, bit in enumerate(order):
        odd = (me // bit) % 2 == 1
        keep, send = cut(value, odd, 0 if i else 1)
        rows = send.shape[0]
        if i and gains is not None:
            got = dp_swap(jnp.concatenate([send, gain_rows(summed, send.shape[1])]), bit)
            summed = gain_sum(summed, got[rows:])
        else:
            got = dp_swap(send, bit)
        value = add_low(keep, got[:rows])
    for i, bit in reversed(list(enumerate(order))):
        odd = (me // bit) % 2 == 1
        rows = value.shape[0]
        if i == 0 and gains is not None:
            got = dp_swap(jnp.concatenate([value, gain_rows(summed, value.shape[1])]), bit)
            summed = gain_sum(summed, got[rows:])
        else:
            got = dp_swap(value, bit)
        value = join(value, got[:rows], odd, 0 if i else 1)
    return value.astype(F32), summed


def doc_positions(marks):
    step_index = jnp.arange(marks.shape[-1], dtype=jnp.int32)
    starts_here = jnp.concatenate([jnp.ones((1,), bool), marks[1:] != marks[:-1]], axis=-1)
    begins = lax.cummax(jnp.where(starts_here, step_index, 0), axis=0)
    return step_index - begins


def rotary_tables(positions):
    half_index = jnp.arange(HEAD_DIM // 2, dtype=F32)
    inverse = jnp.exp(half_index * (-2.0 / HEAD_DIM) * math.log(ROPE_BASE))
    angles = positions.astype(F32)[:, None] * inverse[None, :]
    cosine, sine = jnp.cos(angles), jnp.sin(angles)
    return jnp.concatenate([cosine] * 4, axis=-1), jnp.concatenate([-sine, sine] * 2, axis=-1)


def per_device(
    residual_in,
    segments,
    first_gain,
    packed_weight,
    output_weight,
    second_gain,
    expand_weight,
    reduce_weight,
    upstream,
):
    rows, width = residual_in.shape
    me = lax.axis_index("tensor")
    heads = packed_weight.shape[2] // HEAD_DIM
    units = expand_weight.shape[2]
    barrier = lax.optimization_barrier
    gain_one, gain_two = first_gain[None, :], second_gain[None, :]
    dp_bits = [1 << i for i in range(lax.axis_size("dp").bit_length() - 1)]
    unit_order = dp_bits[1:2] + dp_bits[:1] + dp_bits[2:]

    normal, scale = normal_of(residual_in.astype(F32))
    normed = gather_blocks((normal * gain_one).astype(LOW))
    packed = packed_weight.reshape(width, -1).T
    packed = jnp.pad(packed, ((0, -packed.shape[0] % LANES), (0, 0)))
    expand_own = expand_weight.reshape(width, -1).T

    marks = segments[0]
    positions = doc_positions(marks)
    by_block = lambda row: jnp.concatenate(
        [lax.dynamic_slice_in_dim(row, (me ^ j) * rows, rows, 0) for j in range(4)]
    )
    marks = by_block(marks)[:, None]
    tables = rotary_tables(by_block(positions))
    half = 2 * rows
    halves = [tuple(t[i * half : (i + 1) * half] for t in tables) for i in range(2)]
    near = project(normed[:2], packed, *halves[0], marks[:half], heads)
    normed[2], output_weight, expand_own, reduce_weight, upstream = barrier(
        (normed[2], output_weight, expand_own, reduce_weight, upstream)
    )
    output_all = gather_blocks(output_weight)
    expand_all = gather_blocks(expand_own)
    reduce_all = gather_blocks(reduce_weight)
    upstream_all = gather_blocks(upstream)
    far = project(normed[2:], packed, *halves[1], marks[half:], heads)

    *outs_far, widened_far = attend_forward(far[0], near[1:], far[1:])
    outs_far, near = barrier((outs_far, near))
    *outs_near, widened_near = attend_forward(near[0], near[1:], far[1:])
    mine = [outs_near[0], swap(outs_near[1], 1), swap(outs_far[0], 2), swap(outs_far[1], 3)]
    middle, normed_two = call(
        middle_kernel,
        [((rows, width), F32), ((rows, width), LOW)],
        (*mine, *output_all, residual_in, gain_two),
        2 * rows * width * width,
        "middle",
    )
    normed_two_all = gather_blocks(normed_two)
    residual_out, middle_slope, middle_low, second_part, *slopes = call(
        feed_kernel,
        [((rows, width), F32)] * 2
        + [((rows, width), LOW), ((1, width), F32)]
        + [((rows, heads * HEAD_DIM), LOW)] * 4,
        (*expand_all, *reduce_all, *output_all, middle, normed_two, upstream, gain_two),
        2 * rows * width * (24 * units + width),
        "feed",
    )
    slopes = [slopes[0]] + [swap(slopes[j], j) for j in (1, 2, 3)]
    output_part = call(
        output_sums_kernel,
        [((heads * HEAD_DIM, width), LOW)] * 4,
        (*mine, middle_low),
        2 * rows * width * width,
        "output_sums",
    )
    output_part = scatter_blocks(output_part)
    dq_near, *started = attend_backward(widened_near, near[1:], far[1:], outs_near, slopes[:2], halves[0])
    (unit_part,) = call(
        unit_sums_kernel,
        [((3 * units, width), LOW)],
        (*normed_two_all, *upstream_all, expand_own, reduce_weight),
        2 * rows * width * 24 * units,
        "unit_sums",
        scratch_shapes=[pltpu.VMEM((3 * units, width), F32)],
    )
    unit_part = jnp.concatenate([unit_part, output_part.astype(LOW)])
    unit_part, slopes = barrier((unit_part, slopes))
    unit_sum, _ = dp_sum(unit_part, unit_order)
    dq_far, dk, dv = attend_backward(
        widened_far, near[1:], far[1:], outs_far, slopes[2:], halves[1], started, tables
    )
    packed_part, first_part, *packed_slopes = call(
        partial(packed_sums_kernel, heads),
        [((3 * heads * HEAD_DIM, width), LOW), ((1, width), F32)] + [((rows, packed.shape[0]), LOW)] * 4,
        (dq_near, dq_far, dk, dv, *normed, packed, gain_one),
        8 * rows * width * packed.shape[0],
        "packed_sums",
        scratch_shapes=[pltpu.VMEM(packed.shape, F32)],
    )
    gains = jnp.concatenate([first_part, second_part])
    gains = sum([swap(gains, j) for j in (1, 2, 3)], gains)
    packed_sum, gains = dp_sum(packed_part, dp_bits, gains)
    normed_slope = call(
        normed_slope_kernel,
        [((rows, width), kind) for kind in (F32, LOW, F32, LOW)],
        (*packed_slopes, packed),
        8 * rows * width * packed.shape[0],
        "normed_slope",
    )
    normed_slope = scatter_blocks(normed_slope)
    input_back = middle_slope + norm_pull(normed_slope, normal, scale, gain_one)
    return (
        residual_out,
        input_back,
        gains[0],
        packed_sum.T.reshape(width, 3, -1),
        unit_sum[3 * units :],
        gains[1],
        unit_sum[units : 3 * units].T.reshape(width, 2, units),
        unit_sum[:units],
    )


def solution(mesh):
    rows = P(("dp", "tensor"), None)
    placed = (
        rows,
        P("dp", None),
        P(),
        P(None, None, "tensor"),
        P("tensor", None),
        P(),
        P(None, None, "tensor"),
        P("tensor", None),
        rows,
    )
    return jax.shard_map(
        per_device,
        mesh=mesh,
        in_specs=placed,
        out_specs=(rows, rows, P(), placed[3], placed[4], P(), placed[6], placed[7]),
        check_vma=False,
    )
```

```python
from functools import partial
import math

import jax
import jax.numpy as jnp
from jax import lax
from jax.experimental import pallas as pl
from jax.experimental.pallas import tpu as pltpu
from jax.sharding import PartitionSpec as P

HEAD_DIM = 64
LANES = 128
EPSILON = 1e-05
ROPE_BASE = 160000.0
SCALE = 0.125
MASKED = -1000000000.0
MARKS = 4
MARK_LANE = 64
LOG_LANE = 68
SUM_LANE = 64
MIB = 2**20

F32 = jnp.float32
LOW = jnp.bfloat16
NT = (((1,), (1,)), ((), ()))
TN = (((0,), (0,)), ((), ()))


def dot(left, right):
    return jnp.dot(left, right, preferred_element_type=F32)


def against(left, right):
    return lax.dot_general(left, right, NT, preferred_element_type=F32)


def outer_sum(left, right):
    return lax.dot_general(left, right, TN, preferred_element_type=F32)


def call(kernel, out_shapes, args, flops, name, vmem, **rest):
    shapes = [jax.ShapeDtypeStruct(shape, kind) for shape, kind in out_shapes]
    moved = sum(a.size * a.dtype.itemsize for a in list(args) + shapes)
    return pl.pallas_call(
        kernel,
        out_shape=shapes,
        compiler_params=pltpu.CompilerParams(vmem_limit_bytes=vmem * MIB),
        cost_estimate=pl.CostEstimate(flops=int(flops) // 1000, bytes_accessed=int(moved) // 1000, transcendentals=0),
        name=name,
        **rest,
    )(*args)


def lane_of(shape):
    return lax.broadcasted_iota(jnp.int32, shape, 1)


def split_three(value):
    high = value.astype(LOW)
    rest = value - high.astype(F32)
    middle = rest.astype(LOW)
    return high, middle, (rest - middle.astype(F32)).astype(LOW)


def put_three(base, first, column):
    lane = lane_of(base.shape)
    out = base.astype(F32)
    for step, part in enumerate(split_three(column)):
        out = jnp.where(lane == first + step, part.astype(F32), out)
    return out.astype(LOW)


def rope_lanes(table):
    lane = lane_of(table.shape)
    quarter = HEAD_DIM // 2
    sine = jnp.where((lane >= quarter) & (lane < HEAD_DIM), table, 0.0)
    cosine = jnp.where(lane < quarter, table, 0.0)
    cosine = cosine + pltpu.roll(cosine, quarter, 1)
    sine = sine - pltpu.roll(sine, LANES - quarter, 1)
    return cosine + pltpu.roll(cosine, HEAD_DIM, 1), sine + pltpu.roll(sine, HEAD_DIM, 1)


def head_lanes(head, heads):
    shape = (heads * HEAD_DIM, LANES)
    source = lax.broadcasted_iota(jnp.int32, shape, 0)
    lane = lane_of(shape)
    return jnp.where((lane < HEAD_DIM) & (source == lane + head * HEAD_DIM), 1.0, 0.0).astype(LOW)


def turn_lanes(rows):
    lane = lane_of(rows.shape)
    first = lane % HEAD_DIM < HEAD_DIM // 2
    return jnp.where(first, pltpu.roll(rows, LANES - HEAD_DIM // 2, 1), pltpu.roll(rows, HEAD_DIM // 2, 1))


def packed_lanes(parts):
    keep = lane_of(parts[0].shape) < HEAD_DIM
    tiles = []
    for i in range(0, len(parts), 2):
        left = parts[i].astype(F32)
        right = pltpu.roll(parts[i + 1].astype(F32), HEAD_DIM, 1) if i + 1 < len(parts) else 0.0
        tiles.append(jnp.where(keep, left, right).astype(LOW))
    return jnp.concatenate(tiles, axis=1)


def project_kernel(heads, first, *refs):
    rows_refs, (weight_ref, gain_ref, table_ref) = refs[:2], refs[2:5]
    query_ref, key_ref, value_ref = refs[5:8]
    for b, (rows_ref, normed_ref) in enumerate(zip(rows_refs, refs[8:])):
        rows = rows_ref.shape[0]
        here = pl.ds(b * rows, rows)
        normed = (normal_of(rows_ref[...].astype(F32))[0] * gain_ref[...]).astype(LOW)
        normed_ref[...] = normed
        packed = against(normed, weight_ref[...])
        table = table_ref[pl.ds((first + b) * rows, rows), :]
        cosine, sine = rope_lanes(table)
        lane = lane_of(table.shape)
        upper = lane - MARK_LANE
        same = upper.astype(F32) == table[:, MARK_LANE : MARK_LANE + 1]
        marks = (upper >= 0) & (upper < MARKS)
        logs = (lane >= LOG_LANE) & (lane < LOG_LANE + 3)
        sums = (lane >= SUM_LANE) & (lane < SUM_LANE + 3)
        extras = (
            jnp.where(marks & jnp.logical_not(same), MASKED, 0.0),
            jnp.where((marks & same) | logs, 1.0, 0.0),
            jnp.where(sums, 1.0, 0.0),
        )
        tiles = [packed[:, i : i + LANES] for i in range(0, packed.shape[1], LANES)]
        for i in range(3 * heads):
            rows_part = tiles[i // 2]
            part, head = i // heads, i % heads
            if part < 2:
                rows_part = rows_part * cosine + turn_lanes(rows_part) * sine
            if i % 2 == 1:
                rows_part = pltpu.roll(rows_part, HEAD_DIM, 1)
            if part == 0:
                rows_part = rows_part * SCALE
            out_ref = (query_ref, key_ref, value_ref)[part]
            out_ref[head, here, :] = jnp.where(lane < HEAD_DIM, rows_part, extras[part]).astype(LOW)


def project(blocks, weight, gain, table, heads, start):
    rows, width = blocks[0].shape
    *parts, first, second = call(
        partial(project_kernel, heads, start),
        [((heads, 2 * rows, LANES), LOW)] * 3 + [((rows, width), LOW)] * 2,
        (*blocks, weight, gain, table),
        4 * rows * width * weight.shape[0],
        "project",
        6,
    )
    return parts, [first, second]


def forward_kernel(query_ref, near_key, far_key, near_value, far_value, out_a, out_b, widened_ref):
    heads, half, _ = query_ref.shape
    outs = {0: out_a, half // 2: out_b}
    jobs = [(head, first) for first in outs for head in range(heads)]

    def scores(head, first):
        query = query_ref[head, pl.ds(first, half // 2), :]
        return query, against(query, near_key[head]), against(query, far_key[head])

    following = scores(*jobs[0])
    for i, (head, first) in enumerate(jobs):
        query, near, far = following
        if i + 1 < len(jobs):
            following = scores(*jobs[i + 1])
        top = jnp.maximum(jnp.max(near, axis=1, keepdims=True), jnp.max(far, axis=1, keepdims=True))
        out = dot(jnp.exp(near - top).astype(LOW), near_value[head])
        out = out + dot(jnp.exp(far - top).astype(LOW), far_value[head])
        sums = out[:, SUM_LANE : SUM_LANE + 1]
        widened_ref[head, pl.ds(first, half // 2), :] = put_three(query, LOG_LANE, -(top + jnp.log(sums)))
        part = against((out / sums).astype(LOW), head_lanes(head, heads))
        total = part if head == 0 else total + part
        if head == heads - 1:
            outs[first][...] = total.astype(LOW)


def attend_forward(queries, near, far):
    heads, half, _ = queries.shape
    return call(
        forward_kernel,
        [((half // 2, heads * HEAD_DIM), LOW)] * 2 + [(queries.shape, LOW)],
        (queries, near[0], far[0], near[1], far[1]),
        32 * heads * half * half * HEAD_DIM,
        "attend_forward",
        10,
    )


def backward_kernel(heads, chunk, last, *refs):
    query_ref, near_key, far_key, near_value, far_value, out_a, out_b, slope_a, slope_b = refs[:9]
    table_ref = refs[9]
    if last:
        key_start, value_start = refs[10:12]
    dq_ref, dk_ref, dv_ref = refs[-3:]
    half = query_ref.shape[1]
    pick = head_lanes(pl.program_id(0), heads)
    slope = dot(jnp.concatenate([slope_a[...], slope_b[...]]), pick)
    centre = jnp.sum(slope * dot(jnp.concatenate([out_a[...], out_b[...]]), pick), axis=1, keepdims=True)
    slope = slope.astype(LOW)
    widened = put_three(slope, SUM_LANE, -centre)
    query = query_ref[0]
    keep = lane_of((chunk, LANES)) < HEAD_DIM
    sides = ((near_key, near_value), (far_key, far_value))
    jobs = [(side, first) for side in (0, 1) for first in range(0, half, chunk)]

    def scores(side, first):
        keys = sides[side][0][0, pl.ds(first, chunk), :]
        values = sides[side][1][0, pl.ds(first, chunk), :]
        return keys, against(keys, query), against(values, widened)

    following = scores(*jobs[0])
    total = None
    for i, (side, first) in enumerate(jobs):
        keys, chance, drift = following
        if i + 1 < len(jobs):
            following = scores(*jobs[i + 1])
        here = pl.ds(side * half + first, chunk)
        chance = jnp.exp(chance)
        score_slope = (chance * drift).astype(LOW)
        dv = dot(chance.astype(LOW), slope)
        dk = dot(score_slope, query)
        if last:
            dk = dk + key_start[0, here, :]
            cosine, sine = rope_lanes(table_ref[here, :])
            dk = dk * cosine - turn_lanes(dk) * sine
            dk = jnp.where(keep, dk, 0.0).astype(LOW)
            dv = jnp.where(keep, dv + value_start[0, here, :], 0.0).astype(LOW)
        dk_ref[0, here, :] = dk
        dv_ref[0, here, :] = dv
        part = outer_sum(score_slope, keys)
        total = part if total is None else total + part
    total = total * SCALE
    cosine, sine = rope_lanes(table_ref[pl.ds(half if last else 0, half), :])
    total = total * cosine - turn_lanes(total) * sine
    dq_ref[0] = jnp.where(lane_of(total.shape) < HEAD_DIM, total, 0.0).astype(LOW)


def attend_backward(widened, near, far, outs, slopes, table, started=None):
    heads, half, _ = widened.shape
    head = pl.BlockSpec((1, half, LANES), lambda h: (h, 0, 0))
    long = pl.BlockSpec((1, 2 * half, LANES), lambda h: (h, 0, 0))
    flat = pl.BlockSpec(outs[0].shape, lambda h: (0, 0))
    args = (widened, near[0], far[0], near[1], far[1], *outs, *slopes, table)
    specs = [head] * 5 + [flat] * 4 + [pl.BlockSpec((2 * half, LANES), lambda h: (0, 0))]
    last = started is not None
    if last:
        args += tuple(started)
        specs += [long] * 2
    full = (heads, 2 * half, LANES)
    kind = LOW if last else F32
    return call(
        partial(backward_kernel, heads, half, last),
        [(widened.shape, LOW), (full, kind), (full, kind)],
        args,
        80 * heads * half * half * HEAD_DIM,
        "attend_backward",
        14,
        grid=(heads,),
        in_specs=specs,
        out_specs=[head, long, long],
    )


def mean_of(rows):
    return jnp.mean(rows, axis=-1, keepdims=True)


def normal_of(rows):
    center = rows - mean_of(rows)
    scale = lax.rsqrt(mean_of(center * center) + EPSILON)
    return center * scale, scale


def norm_pull(slope, normal, scale, gain):
    inner = slope * gain
    return scale * (inner - mean_of(inner) - normal * mean_of(inner * normal))


def middle_kernel(*refs):
    attended, weights, (rows_ref, gain_ref, middle_ref, normed_ref) = refs[:4], refs[4:8], refs[8:]
    middle = rows_ref[...].astype(F32)
    for attended_ref, weight_ref in zip(attended, weights):
        middle = middle + dot(attended_ref[...], weight_ref[: attended_ref.shape[1], :])
    middle_ref[...] = middle
    normed_ref[...] = (normal_of(middle)[0] * gain_ref[...]).astype(LOW)


def gelu_parts(gate):
    bell = 0.5 * (1.0 + lax.erf(gate * math.sqrt(0.5)))
    slope = bell + gate * jnp.exp(-0.5 * gate * gate) * (1.0 / math.sqrt(2.0 * math.pi))
    return gate * bell, slope


def gated(gate, up, hidden_slope):
    active, active_slope = gelu_parts(gate)
    hidden = (active * up).astype(LOW)
    return hidden, (hidden_slope * up * active_slope).astype(LOW), (hidden_slope * active).astype(LOW)


def stacked(refs):
    return jnp.concatenate([ref[...] for ref in refs])


def feed_kernel(*refs):
    first, second = refs[:4], refs[4:8]
    attended, (middle_ref, normed_ref, upstream_ref, gain_ref) = refs[8:12], refs[12:16]
    out_ref, slope_ref, gain_sum_ref = refs[16:19]
    units = second[0].shape[0] // 2
    skip = first[0].shape[0] - units
    gate_weight = jnp.concatenate([ref[skip:, :] for ref in first])
    up_weight = jnp.concatenate([ref[:units, :] for ref in second])
    reduce = jnp.concatenate([ref[units:, :] for ref in second])
    middle, normed, upstream = middle_ref[...], normed_ref[...], upstream_ref[...]
    hidden, gate_slope, up_slope = gated(
        against(normed, gate_weight), against(normed, up_weight), against(upstream, reduce)
    )
    normed_slope = dot(gate_slope, gate_weight) + dot(up_slope, up_weight)
    normal, scale = normal_of(middle)
    slope = upstream.astype(F32) + norm_pull(normed_slope, normal, scale, gain_ref[...])
    slope_ref[...] = slope
    low = slope.astype(LOW)
    for weight_ref, attended_ref, attended_slope_ref, sum_ref in zip(first, attended, refs[19:23], refs[23:]):
        attended_slope_ref[...] = against(low, weight_ref[:skip, :]).astype(LOW)
        sum_ref[...] = outer_sum(attended_ref[...], low).astype(LOW)
    gain_sum_ref[...] = jnp.sum(normed_slope * normal, axis=0, keepdims=True)
    out_ref[...] = middle + dot(hidden, reduce)


def unit_sums_kernel(*refs):
    normed, upstream, (first_ref, second_ref, out_ref) = stacked(refs[:4]), stacked(refs[4:8]), refs[8:]
    units = second_ref.shape[0] // 2
    parts = gated(
        against(first_ref[first_ref.shape[0] - units :, :], normed),
        against(second_ref[:units, :], normed),
        against(second_ref[units:, :], upstream),
    )
    for i, (part, other) in enumerate(zip(parts, (upstream, normed, normed))):
        out_ref[pl.ds(i * units, units), :] = dot(part, other).astype(LOW)


def packed_sums_kernel(heads, *refs):
    dq_a, dq_b, dk, dv, normed, (weight_ref, gain_ref) = *refs[:4], refs[4:8], refs[8:10]
    out_ref, gain_sum_ref, slope_refs, total_ref = refs[10], refs[11], refs[12:16], refs[16]
    rows = normed[0].shape[0]
    used = out_ref.shape[0]
    for b in range(4):
        here = pl.ds(b * rows, rows)
        dq = dq_a if b < 2 else dq_b
        parts = [dq[h, pl.ds((b % 2) * rows, rows), :] for h in range(heads)]
        parts += [ref[h, here, :] for ref in (dk, dv) for h in range(heads)]
        slope = packed_lanes(parts)
        slope_refs[b][...] = slope
        total = outer_sum(slope, normed[b][...])
        total_ref[...] = total if b == 0 else total_ref[...] + total
    total = total_ref[:used, :]
    out_ref[...] = total.astype(LOW)
    weight = weight_ref[:used, :].astype(F32)
    gain_sum_ref[...] = jnp.sum(total * weight, axis=0, keepdims=True) / gain_ref[...]


def normed_slope_kernel(*refs):
    slopes, weight_ref, outs = refs[:4], refs[4], refs[5:]
    for slope_ref, out_ref in zip(slopes, outs):
        out_ref[...] = dot(slope_ref[...], weight_ref[...]).astype(out_ref.dtype)


def swap(value, offset):
    size = lax.axis_size("tensor")
    return lax.ppermute(value, "tensor", [(i, i ^ offset) for i in range(size)])


def dp_swap(value, offset):
    size = lax.axis_size("dp")
    return lax.ppermute(value, "dp", [(i, i ^ offset) for i in range(size)])


def scatter_blocks(blocks):
    near = blocks[0].astype(F32) + swap(blocks[1], 1).astype(F32)
    far = blocks[2].astype(F32) + swap(blocks[3], 1).astype(F32)
    return near + swap(far.astype(LOW), 2).astype(F32)


def add_low(left, right):
    return (left.astype(F32) + right.astype(F32)).astype(LOW)


def cut(value, odd, axis):
    half = value.shape[axis] // 2
    lower, upper = (lax.slice_in_dim(value, i * half, (i + 1) * half, axis=axis) for i in range(2))
    return jnp.where(odd, upper, lower), jnp.where(odd, lower, upper)


def join(value, got, odd, axis):
    return jnp.concatenate([jnp.where(odd, got, value), jnp.where(odd, value, got)], axis=axis)


def gain_rows(gains, columns):
    rows = jnp.concatenate(split_three(gains)).reshape(-1, columns)
    return jnp.pad(rows, ((0, -rows.shape[0] % 16), (0, 0)))


def gain_sum(gains, rows):
    parts = rows[: 3 * gains.size // rows.shape[1]].reshape((3,) + gains.shape).astype(F32)
    return gains + parts[0] + parts[1] + parts[2]


class DpSum:
    def __init__(self, value, order, gains=None):
        self.value, self.gains = value, gains
        self.todo = [(bit, 0 if i else 1, True) for i, bit in enumerate(order)]
        self.todo += [(bit, axis, False) for bit, axis, _ in reversed(self.todo)]

    def step(self):
        bit, axis, scatter = self.todo.pop(0)
        odd = (lax.axis_index("dp") // bit) % 2 == 1
        keep, send = cut(self.value, odd, axis) if scatter else (self.value, self.value)
        rows = send.shape[0]
        riding = self.gains is not None and scatter == (axis == 0)
        if riding:
            send = jnp.concatenate([send, gain_rows(self.gains, send.shape[1])])
        got = dp_swap(send, bit)
        if riding:
            self.gains = gain_sum(self.gains, got[rows:])
        got = got[:rows]
        self.value = add_low(keep, got) if scatter else join(keep, got, odd, axis)

    def finish(self):
        while self.todo:
            self.step()
        return self.value.astype(F32), self.gains


def in_step(first, second):
    first.value, second.value = lax.optimization_barrier((first.value, second.value))


def doc_positions(marks):
    step_index = jnp.arange(marks.shape[-1], dtype=jnp.int32)
    starts_here = jnp.concatenate([jnp.ones((1,), bool), marks[1:] != marks[:-1]], axis=-1)
    begins = lax.cummax(jnp.where(starts_here, step_index, 0), axis=0)
    return step_index - begins


def row_table(positions, marks):
    half_index = jnp.arange(HEAD_DIM // 2, dtype=F32)
    inverse = jnp.exp(half_index * (-2.0 / HEAD_DIM) * math.log(ROPE_BASE))
    angles = positions.astype(F32)[:, None] * inverse[None, :]
    mark = jnp.broadcast_to(marks.astype(F32)[:, None], (marks.shape[0], HEAD_DIM))
    return jnp.concatenate([jnp.cos(angles), jnp.sin(angles), mark], axis=-1)


def per_device(
    residual_in,
    segments,
    first_gain,
    packed_weight,
    output_weight,
    second_gain,
    expand_weight,
    reduce_weight,
    upstream,
):
    rows, width = residual_in.shape
    me = lax.axis_index("tensor")
    heads = packed_weight.shape[2] // HEAD_DIM
    units = expand_weight.shape[2]
    barrier = lax.optimization_barrier
    gain_one, gain_two = first_gain[None, :], second_gain[None, :]
    dp_bits = [1 << i for i in range(lax.axis_size("dp").bit_length() - 1)]
    dp_bits[:2] = dp_bits[1::-1]

    packed = packed_weight.reshape(width, -1).T
    packed = jnp.pad(packed, ((0, -packed.shape[0] % LANES), (0, 0)))
    from_core = swap(residual_in, 1)
    from_chip = swap(residual_in, 2)

    marks = segments[0]
    positions = doc_positions(marks)
    by_block = lambda row: jnp.concatenate(
        [lax.dynamic_slice_in_dim(row, (me ^ j) * rows, rows, 0) for j in range(4)]
    )
    table = row_table(by_block(positions), by_block(marks))
    near, normed = project([residual_in, from_core], packed, gain_one, table, heads, 0)
    weights = [
        jnp.concatenate([output_weight, expand_weight[:, 0].T]),
        jnp.concatenate([expand_weight[:, 1].T, reduce_weight]),
    ]
    from_chip, near, weights = barrier((from_chip, near, weights))
    far, normed_far = project(
        [from_chip, swap(from_chip, 1)], packed, gain_one, table, heads, 2
    )
    normed = normed + normed_far

    odd = lax.axis_index("dp") % 2 == 1
    got = [swap(cut(w, odd, 0)[0], 2) for w in weights]
    from_core = [swap(w, 1) for w in weights]
    *outs_far, widened_far = attend_forward(far[0], near[1:], far[1:])
    outs_far, near, got[0] = barrier((outs_far, near, got[0]))
    got_first = dp_swap(got[0], 1)
    *outs_near, widened_near = attend_forward(near[0], near[1:], far[1:])
    outs_near, *got, got_first, upstream_sent = barrier((outs_near, *got, got_first, upstream))
    chip_first = join(got[0], got_first, odd, 0)
    got_second = dp_swap(got[1], 1)
    mine = [outs_near[0], swap(outs_near[1], 1), swap(outs_far[0], 2), swap(outs_far[1], 3)]
    upstream_all = [upstream, swap(upstream, 1), swap(upstream_sent, 2)]
    all_first = [weights[0], from_core[0], chip_first, swap(chip_first, 1)]
    middle, normed_two = call(
        middle_kernel,
        [((rows, width), F32), ((rows, width), LOW)],
        (*mine, *all_first, residual_in, gain_two),
        2 * rows * width * width,
        "middle",
        6,
    )
    normed_two, *got_second = barrier((normed_two, got[1], got_second))
    chip_second = join(*got_second, odd, 0)
    all_second = [weights[1], from_core[1], chip_second, swap(chip_second, 1)]
    normed_two_all = [normed_two, swap(normed_two, 1), swap(normed_two, 2)]
    residual_out, middle_slope, second_part, *slopes = call(
        feed_kernel,
        [((rows, width), F32)] * 2
        + [((1, width), F32)]
        + [((rows, heads * HEAD_DIM), LOW)] * 4
        + [((heads * HEAD_DIM, width), LOW)] * 4,
        (*all_first, *all_second, *mine, middle, normed_two, upstream, gain_two),
        2 * rows * width * (24 * units + 2 * width),
        "feed",
        16,
    )
    slopes, output_part = slopes[:4], slopes[4:]
    slopes = [slopes[0]] + [swap(slopes[j], j) for j in (1, 2, 3)]
    from_core_sums = [swap(output_part[1], 1), swap(output_part[3], 1)]
    dq_near, *started = attend_backward(widened_near, near[1:], far[1:], outs_near, slopes[:2], table)
    started, normed_two_all, upstream_all, from_core_sums = barrier(
        (started, normed_two_all, upstream_all, from_core_sums)
    )
    normed_two_all.append(swap(normed_two_all[2], 1))
    upstream_all.append(swap(upstream_all[2], 1))
    output_near = add_low(output_part[0], from_core_sums[0])
    output_far = swap(add_low(output_part[2], from_core_sums[1]), 2)
    (unit_part,) = call(
        unit_sums_kernel,
        [((3 * units, width), LOW)],
        (*normed_two_all, *upstream_all, *weights),
        48 * units * width * rows,
        "unit_sums",
        14,
    )
    unit_part, output_far = barrier((unit_part, output_far))
    unit_part = jnp.concatenate([unit_part, add_low(output_near, output_far)])
    unit_sum = DpSum(unit_part, dp_bits)
    unit_sum.value, slopes[2:] = barrier((unit_sum.value, slopes[2:]))
    unit_sum.step()
    dq_far, dk, dv = attend_backward(
        widened_far, near[1:], far[1:], outs_far, slopes[2:], table, started
    )
    dq_far, unit_sum.value = barrier((dq_far, unit_sum.value))
    unit_sum.step()
    packed_part, first_part, *packed_slopes = call(
        partial(packed_sums_kernel, heads),
        [((3 * heads * HEAD_DIM, width), LOW), ((1, width), F32)] + [((rows, packed.shape[0]), LOW)] * 4,
        (dq_near, dq_far, dk, dv, *normed, packed, gain_one),
        8 * rows * width * packed.shape[0],
        "packed_sums",
        10,
        scratch_shapes=[pltpu.VMEM(packed.shape, F32)],
    )
    gains = jnp.concatenate([first_part, second_part])
    gains = sum([swap(gains, j) for j in (1, 2, 3)], gains)
    packed_sum = DpSum(packed_part, dp_bits, gains)
    packed_sum.step()
    normed_slope = call(
        normed_slope_kernel,
        [((rows, width), kind) for kind in (F32, LOW, F32, LOW)],
        (*packed_slopes, packed),
        8 * rows * width * packed.shape[0],
        "normed_slope",
        6,
    )
    normed_slope = scatter_blocks(normed_slope)
    normal, scale = normal_of(residual_in.astype(F32))
    input_back = middle_slope + norm_pull(normed_slope, normal, scale, gain_one)
    packed_sum, gains = packed_sum.finish()
    unit_sum, _ = unit_sum.finish()
    return (
        residual_out,
        input_back,
        gains[0],
        packed_sum.T.reshape(width, 3, -1),
        unit_sum[3 * units :],
        gains[1],
        unit_sum[units : 3 * units].T.reshape(width, 2, units),
        unit_sum[:units],
    )


def solution(mesh):
    rows = P(("dp", "tensor"), None)
    placed = (
        rows,
        P("dp", None),
        P(),
        P(None, None, "tensor"),
        P("tensor", None),
        P(),
        P(None, None, "tensor"),
        P("tensor", None),
        rows,
    )
    return jax.shard_map(
        per_device,
        mesh=mesh,
        in_specs=placed,
        out_specs=(rows, rows, P(), placed[3], placed[4], P(), placed[6], placed[7]),
        check_vma=False,
    )
```

```python
from functools import partial
import math

import jax
import jax.numpy as jnp
from jax import lax
from jax.experimental import pallas as pl
from jax.experimental.pallas import tpu as pltpu
from jax.sharding import PartitionSpec as P

HEAD_DIM = 64
LANES = 128
EPSILON = 1e-05
ROPE_BASE = 160000.0
SCALE = 0.125
MASKED = -1000000000.0
MARKS = 4
MARK_LANE = 64
LOG_LANE = 68
SUM_LANE = 64
MIB = 2**20

F32 = jnp.float32
LOW = jnp.bfloat16
NT = (((1,), (1,)), ((), ()))
TN = (((0,), (0,)), ((), ()))


def dot(left, right):
    return jnp.dot(left, right, preferred_element_type=F32)


def against(left, right):
    return lax.dot_general(left, right, NT, preferred_element_type=F32)


def outer_sum(left, right):
    return lax.dot_general(left, right, TN, preferred_element_type=F32)


def pause_kernel(value_ref, out_ref):
    out_ref[...] = jnp.zeros_like(out_ref)


def pause(value):
    return pl.pallas_call(
        pause_kernel,
        in_specs=[pl.BlockSpec(memory_space=pl.ANY)],
        out_shape=jax.ShapeDtypeStruct((8, LANES), F32),
        cost_estimate=pl.CostEstimate(flops=10**12, bytes_accessed=10**9, transcendentals=0),
        name="pause",
    )(value)


def call(kernel, out_shapes, args, flops, name, vmem, outside=(), **rest):
    shapes = [
        (pltpu.HBM if i in outside else jax.ShapeDtypeStruct)(shape, kind)
        for i, (shape, kind) in enumerate(out_shapes)
    ]
    moved = sum(math.prod(a.shape) * jnp.dtype(a.dtype).itemsize for a in list(args) + shapes)
    return pl.pallas_call(
        kernel,
        out_shape=shapes,
        compiler_params=pltpu.CompilerParams(vmem_limit_bytes=vmem * MIB),
        cost_estimate=pl.CostEstimate(flops=int(flops) // 1000, bytes_accessed=int(moved) // 1000, transcendentals=0),
        name=name,
        **rest,
    )(*args)


def lane_of(shape):
    return lax.broadcasted_iota(jnp.int32, shape, 1)


def split_three(value):
    high = value.astype(LOW)
    rest = value - high.astype(F32)
    middle = rest.astype(LOW)
    return high, middle, (rest - middle.astype(F32)).astype(LOW)


def put_three(base, first, column):
    lane = lane_of(base.shape)
    out = base.astype(F32)
    for step, part in enumerate(split_three(column)):
        out = jnp.where(lane == first + step, part.astype(F32), out)
    return out.astype(LOW)


def rope_lanes(table):
    lane = lane_of(table.shape)
    quarter = HEAD_DIM // 2
    sine = jnp.where((lane >= quarter) & (lane < HEAD_DIM), table, 0.0)
    cosine = jnp.where(lane < quarter, table, 0.0)
    cosine = cosine + pltpu.roll(cosine, quarter, 1)
    sine = sine - pltpu.roll(sine, LANES - quarter, 1)
    return cosine + pltpu.roll(cosine, HEAD_DIM, 1), sine + pltpu.roll(sine, HEAD_DIM, 1)


def head_lanes(head, heads):
    shape = (heads * HEAD_DIM, LANES)
    source = lax.broadcasted_iota(jnp.int32, shape, 0)
    lane = lane_of(shape)
    return jnp.where((lane < HEAD_DIM) & (source == lane + head * HEAD_DIM), 1.0, 0.0).astype(LOW)


def turn_lanes(rows):
    lane = lane_of(rows.shape)
    first = lane % HEAD_DIM < HEAD_DIM // 2
    return jnp.where(first, pltpu.roll(rows, LANES - HEAD_DIM // 2, 1), pltpu.roll(rows, HEAD_DIM // 2, 1))


def packed_lanes(parts):
    keep = lane_of(parts[0].shape) < HEAD_DIM
    tiles = []
    for i in range(0, len(parts), 2):
        left = parts[i].astype(F32)
        right = pltpu.roll(parts[i + 1].astype(F32), HEAD_DIM, 1) if i + 1 < len(parts) else 0.0
        tiles.append(jnp.where(keep, left, right).astype(LOW))
    return jnp.concatenate(tiles, axis=1)


def project_kernel(heads, first, *refs):
    rows_refs, (weight_ref, gain_ref, table_ref) = refs[:2], refs[2:5]
    query_ref, key_ref, value_ref = refs[5:8]
    for b, rows_ref in enumerate(rows_refs):
        rows = rows_ref.shape[0]
        here = pl.ds(b * rows, rows)
        normed = (normal_of(rows_ref[...].astype(F32))[0] * gain_ref[...]).astype(LOW)
        packed = against(normed, weight_ref[...])
        table = table_ref[pl.ds((first + b) * rows, rows), :]
        cosine, sine = rope_lanes(table)
        lane = lane_of(table.shape)
        upper = lane - MARK_LANE
        same = upper.astype(F32) == table[:, MARK_LANE : MARK_LANE + 1]
        marks = (upper >= 0) & (upper < MARKS)
        logs = (lane >= LOG_LANE) & (lane < LOG_LANE + 3)
        sums = (lane >= SUM_LANE) & (lane < SUM_LANE + 3)
        extras = (
            jnp.where(marks & jnp.logical_not(same), MASKED, 0.0),
            jnp.where((marks & same) | logs, 1.0, 0.0),
            jnp.where(sums, 1.0, 0.0),
        )
        tiles = [packed[:, i : i + LANES] for i in range(0, packed.shape[1], LANES)]
        for i in range(3 * heads):
            rows_part = tiles[i // 2]
            part, head = i // heads, i % heads
            if part < 2:
                rows_part = rows_part * cosine + turn_lanes(rows_part) * sine
            if i % 2 == 1:
                rows_part = pltpu.roll(rows_part, HEAD_DIM, 1)
            if part == 0:
                rows_part = rows_part * SCALE
            out_ref = (query_ref, key_ref, value_ref)[part]
            out_ref[head, here, :] = jnp.where(lane < HEAD_DIM, rows_part, extras[part]).astype(LOW)


def project(blocks, weight, gain, table, heads, start):
    rows, width = blocks[0].shape
    return call(
        partial(project_kernel, heads, start),
        [((heads, 2 * rows, LANES), LOW)] * 3,
        (*blocks, weight, gain, table),
        4 * rows * width * weight.shape[0],
        "project",
        6,
    )


def forward_kernel(blocks, query_ref, near_key, far_key, near_value, far_value, *refs):
    heads, half, _ = query_ref.shape
    widened_ref = refs[-1]
    outs = {block * (half // 2): ref for block, ref in zip(blocks, refs)}
    jobs = [(head, first) for first in outs for head in range(heads)]

    def scores(head, first):
        query = query_ref[head, pl.ds(first, half // 2), :]
        return query, against(query, near_key[head]), against(query, far_key[head])

    following = scores(*jobs[0])
    for i, (head, first) in enumerate(jobs):
        query, near, far = following
        if i + 1 < len(jobs):
            following = scores(*jobs[i + 1])
        top = jnp.maximum(jnp.max(near, axis=1, keepdims=True), jnp.max(far, axis=1, keepdims=True))
        out = dot(jnp.exp(near - top).astype(LOW), near_value[head])
        out = out + dot(jnp.exp(far - top).astype(LOW), far_value[head])
        sums = out[:, SUM_LANE : SUM_LANE + 1]
        place = first - min(outs)
        widened_ref[head, pl.ds(place, half // 2), :] = put_three(query, LOG_LANE, -(top + jnp.log(sums)))
        part = against((out / sums).astype(LOW), head_lanes(head, heads))
        total = part if head == 0 else total + part
        if head == heads - 1:
            outs[first][...] = total.astype(LOW)


def attend_forward(queries, near, far, blocks):
    heads, half, _ = queries.shape
    rows = half // 2
    return call(
        partial(forward_kernel, blocks),
        [((rows, heads * HEAD_DIM), LOW)] * len(blocks) + [((heads, len(blocks) * rows, LANES), LOW)],
        (queries, near[0], far[0], near[1], far[1]),
        16 * heads * half * half * HEAD_DIM * len(blocks),
        "attend_forward",
        9,
    )


def backward_kernel(heads, chunk, last, *refs):
    near_key, far_key, near_value, far_value, out_a, out_b, slope_a, slope_b, table_ref = refs[:9]
    key_start, value_start = refs[9:11] if last else (None, None)
    queries = refs[11:-3] if last else refs[9:-3]
    dq_ref, dk_ref, dv_ref = refs[-3:]
    half = near_key.shape[1]
    pick = head_lanes(pl.program_id(0), heads)
    slope = dot(jnp.concatenate([slope_a[...], slope_b[...]]), pick)
    centre = jnp.sum(slope * dot(jnp.concatenate([out_a[...], out_b[...]]), pick), axis=1, keepdims=True)
    slope = slope.astype(LOW)
    widened = put_three(slope, SUM_LANE, -centre)
    query = jnp.concatenate([ref[0] for ref in queries])
    keep = lane_of((chunk, LANES)) < HEAD_DIM
    sides = ((near_key, near_value), (far_key, far_value))
    jobs = [(side, first) for side in (0, 1) for first in range(0, half, chunk)]

    def scores(side, first):
        keys = sides[side][0][0, pl.ds(first, chunk), :]
        values = sides[side][1][0, pl.ds(first, chunk), :]
        return keys, against(keys, query), against(values, widened)

    following = scores(*jobs[0])
    total = None
    for i, (side, first) in enumerate(jobs):
        keys, chance, drift = following
        if i + 1 < len(jobs):
            following = scores(*jobs[i + 1])
        here = pl.ds(side * half + first, chunk)
        chance = jnp.exp(chance)
        score_slope = (chance * drift).astype(LOW)
        dv = dot(chance.astype(LOW), slope)
        dk = dot(score_slope, query)
        if last:
            dk = dk + key_start[0, here, :].astype(F32)
            cosine, sine = rope_lanes(table_ref[here, :])
            dk = dk * cosine - turn_lanes(dk) * sine
            dk = jnp.where(keep, dk, 0.0)
            dv = jnp.where(keep, dv + value_start[0, here, :].astype(F32), 0.0)
        dk_ref[0, here, :] = dk.astype(LOW)
        dv_ref[0, here, :] = dv.astype(LOW)
        part = outer_sum(score_slope, keys)
        total = part if total is None else total + part
    total = total * SCALE
    cosine, sine = rope_lanes(table_ref[pl.ds(half if last else 0, half), :])
    total = total * cosine - turn_lanes(total) * sine
    dq_ref[0] = jnp.where(lane_of(total.shape) < HEAD_DIM, total, 0.0).astype(LOW)


def attend_backward(widened, near, far, outs, slopes, table, started=None):
    heads, half, _ = near[0].shape
    head = pl.BlockSpec((1, half, LANES), lambda h: (h, 0, 0))
    long = pl.BlockSpec((1, 2 * half, LANES), lambda h: (h, 0, 0))
    flat = pl.BlockSpec(outs[0].shape, lambda h: (0, 0))
    args = (near[0], far[0], near[1], far[1])
    if started is None:
        args = tuple(pltpu.with_memory_space_constraint(rows, pltpu.HBM) for rows in args)
    args += (*outs, *slopes, table)
    specs = [head] * 4 + [flat] * 4 + [pl.BlockSpec((2 * half, LANES), lambda h: (0, 0))]
    last = started is not None
    if last:
        args += tuple(started)
        specs += [long] * 2
    args += tuple(widened)
    specs += [pl.BlockSpec((1, rows.shape[1], LANES), lambda h: (h, 0, 0)) for rows in widened]
    full = (heads, 2 * half, LANES)
    return call(
        partial(backward_kernel, heads, half, last),
        [((heads, half, LANES), LOW), (full, LOW), (full, LOW)],
        args,
        80 * heads * half * half * HEAD_DIM,
        "attend_backward",
        12,
        grid=(heads,),
        in_specs=specs,
        out_specs=[head, long, long],
    )


def mean_of(rows):
    return jnp.mean(rows, axis=-1, keepdims=True)


def normal_of(rows):
    center = rows - mean_of(rows)
    scale = lax.rsqrt(mean_of(center * center) + EPSILON)
    return center * scale, scale


def norm_pull(slope, normal, scale, gain):
    inner = slope * gain
    return scale * (inner - mean_of(inner) - normal * mean_of(inner * normal))


def middle_kernel(*refs):
    attended, weights, (rows_ref, gain_ref, middle_ref, normed_ref) = refs[:4], refs[4:8], refs[8:]
    middle = rows_ref[...].astype(F32)
    for attended_ref, weight_ref in zip(attended, weights):
        middle = middle + dot(attended_ref[...], weight_ref[: attended_ref.shape[1], :])
    middle_ref[...] = middle
    normed_ref[...] = (normal_of(middle)[0] * gain_ref[...]).astype(LOW)


def gelu_parts(gate):
    bell = 0.5 * (1.0 + lax.erf(gate * math.sqrt(0.5)))
    slope = bell + gate * jnp.exp(-0.5 * gate * gate) * (1.0 / math.sqrt(2.0 * math.pi))
    return gate * bell, slope


def gated(gate, up, hidden_slope):
    active, active_slope = gelu_parts(gate)
    hidden = (active * up).astype(LOW)
    return hidden, (hidden_slope * up * active_slope).astype(LOW), (hidden_slope * active).astype(LOW)


def stacked(refs):
    return jnp.concatenate([ref[...] for ref in refs])


def feed_kernel(*refs):
    first, second = refs[:4], refs[4:8]
    attended, (middle_ref, normed_ref, upstream_ref, gain_ref) = refs[8:12], refs[12:16]
    out_ref, slope_ref, gain_sum_ref = refs[16:19]
    units = second[0].shape[0] // 2
    skip = first[0].shape[0] - units
    gate_weight = jnp.concatenate([ref[skip:, :] for ref in first])
    up_weight = jnp.concatenate([ref[:units, :] for ref in second])
    reduce = jnp.concatenate([ref[units:, :] for ref in second])
    middle, normed, upstream = middle_ref[...], normed_ref[...], upstream_ref[...]
    hidden, gate_slope, up_slope = gated(
        against(normed, gate_weight), against(normed, up_weight), against(upstream, reduce)
    )
    normed_slope = dot(gate_slope, gate_weight) + dot(up_slope, up_weight)
    normal, scale = normal_of(middle)
    slope = upstream.astype(F32) + norm_pull(normed_slope, normal, scale, gain_ref[...])
    slope_ref[...] = slope
    low = slope.astype(LOW)
    for weight_ref, attended_ref, attended_slope_ref, sum_ref in zip(first, attended, refs[19:23], refs[23:]):
        attended_slope_ref[...] = against(low, weight_ref[:skip, :]).astype(LOW)
        sum_ref[...] = outer_sum(attended_ref[...], low).astype(LOW)
    gain_sum_ref[...] = jnp.sum(normed_slope * normal, axis=0, keepdims=True)
    out_ref[...] = middle + dot(hidden, reduce)


def unit_sums_kernel(*refs):
    normed, upstream, (first_ref, second_ref, out_ref) = stacked(refs[:4]), stacked(refs[4:8]), refs[8:]
    units = second_ref.shape[0] // 2
    parts = gated(
        against(first_ref[first_ref.shape[0] - units :, :], normed),
        against(second_ref[:units, :], normed),
        against(second_ref[units:, :], upstream),
    )
    for i, (part, other) in enumerate(zip(parts, (upstream, normed, normed))):
        out_ref[pl.ds(i * units, units), :] = dot(part, other).astype(LOW)


def packed_sums_kernel(heads, *refs):
    dq_a, dq_b, dk, dv, blocks, (weight_ref, gain_ref) = *refs[:4], refs[4:8], refs[8:10]
    out_ref, gain_sum_ref, slope_refs, total_ref = refs[10], refs[11], refs[12:16], refs[16]
    rows = blocks[0].shape[0]
    used = out_ref.shape[0]
    for b in range(4):
        here = pl.ds(b * rows, rows)
        dq = dq_a if b < 2 else dq_b
        parts = [dq[h, pl.ds((b % 2) * rows, rows), :] for h in range(heads)]
        parts += [ref[h, here, :] for ref in (dk, dv) for h in range(heads)]
        slope = packed_lanes(parts)
        slope_refs[b][...] = slope
        normed = (normal_of(blocks[b][...].astype(F32))[0] * gain_ref[...]).astype(LOW)
        total = outer_sum(slope, normed)
        total_ref[...] = total if b == 0 else total_ref[...] + total
    total = total_ref[:used, :]
    out_ref[...] = total.astype(LOW)
    weight = weight_ref[:used, :].astype(F32)
    gain_sum_ref[...] = jnp.sum(total * weight, axis=0, keepdims=True) / gain_ref[...]


def normed_slope_kernel(*refs):
    slopes, weight_ref, outs = refs[:4], refs[4], refs[5:]
    for slope_ref, out_ref in zip(slopes, outs):
        out_ref[...] = dot(slope_ref[...], weight_ref[...]).astype(out_ref.dtype)


def swap(value, offset):
    size = lax.axis_size("tensor")
    return lax.ppermute(value, "tensor", [(i, i ^ offset) for i in range(size)])


def dp_swap(value, offset):
    size = lax.axis_size("dp")
    return lax.ppermute(value, "dp", [(i, i ^ offset) for i in range(size)])


def place_kernel(odd_ref, mine_ref, other_ref, out_ref):
    rows = mine_ref.shape[0]
    odd = odd_ref[0]

    @pl.when(odd == 0)
    def _():
        out_ref[:rows, :] = mine_ref[...]
        out_ref[rows:, :] = other_ref[...]

    @pl.when(odd == 1)
    def _():
        out_ref[:rows, :] = other_ref[...]
        out_ref[rows:, :] = mine_ref[...]


def place(mine, other):
    rows, width = mine.shape
    odd = (lax.axis_index("dp") % 2).astype(jnp.int32).reshape(1)
    whole = pl.BlockSpec(mine.shape, lambda: (0, 0))
    (out,) = call(
        place_kernel,
        [((2 * rows, width), LOW)],
        (odd, mine, other),
        0,
        "place",
        6,
        in_specs=[pl.BlockSpec(memory_space=pltpu.SMEM), whole, whole],
    )
    return out


def add_low(left, right):
    return (left.astype(F32) + right.astype(F32)).astype(LOW)


def cut(value, odd, axis):
    half = value.shape[axis] // 2
    lower, upper = (lax.slice_in_dim(value, i * half, (i + 1) * half, axis=axis) for i in range(2))
    return jnp.where(odd, upper, lower), jnp.where(odd, lower, upper)


def join(value, got, odd, axis):
    return jnp.concatenate([jnp.where(odd, got, value), jnp.where(odd, value, got)], axis=axis)


def gain_rows(gains, columns):
    rows = jnp.concatenate(split_three(gains)).reshape(-1, columns)
    return jnp.pad(rows, ((0, -rows.shape[0] % 16), (0, 0)))


def gain_sum(gains, rows):
    parts = rows[: 3 * gains.size // rows.shape[1]].reshape((3,) + gains.shape).astype(F32)
    return gains + parts[0] + parts[1] + parts[2]


def join_four(parts, place):
    odd, high = place % 2 == 1, place // 2 == 1
    return join(join(parts[0], parts[1], odd, 0), join(parts[2], parts[3], odd, 0), high, 0)


class DpSum:
    def __init__(self, value, gains=None):
        self.value, self.gains, self.me = value, gains, lax.axis_index("dp")
        pairs = [1 << i for i in range(2, lax.axis_size("dp").bit_length() - 1)]
        pairs = [(bit, 0 if i else 1) for i, bit in enumerate(pairs)]
        self.todo = ["scatter"] + pairs + [(bit, axis + 2) for bit, axis in reversed(pairs)] + ["gather"]

    def send(self):
        step = self.todo[0]
        place = self.me % 4
        self.rides = self.gains is not None and step != "scatter" and (step == "gather" or step[1] < 2)
        if step == "scatter":
            rows = self.value.shape[0] // 4
            parts = [lax.dynamic_slice_in_dim(self.value, (place ^ j) * rows, rows, 0) for j in range(4)]
            self.keep, sent, bits = parts[0], parts[1:], (1, 2, 3)
        elif step == "gather":
            self.keep, sent, bits = self.value, [self.value] * 3, (1, 2, 3)
        else:
            bits, self.odd = step[:1], (self.me // step[0]) % 2 == 1
            self.keep, send = cut(self.value, self.odd, step[1]) if step[1] < 2 else (self.value, self.value)
            sent = [send]
        if self.rides:
            riders = gain_rows(self.gains, sent[0].shape[1])
            sent = [jnp.concatenate([part, riders]) for part in sent]
        self.got = [dp_swap(part, bit) for part, bit in zip(sent, bits)]

    def receive(self):
        step = self.todo.pop(0)
        rows = self.keep.shape[0]
        if self.rides:
            for part in self.got:
                self.gains = gain_sum(self.gains, part[rows:])
        got = [part[:rows] for part in self.got]
        if step == "scatter":
            self.value = sum([part.astype(F32) for part in got], self.keep.astype(F32)).astype(LOW)
        elif step == "gather":
            self.value = join_four([self.keep] + got, self.me % 4)
        elif step[1] < 2:
            self.value = add_low(self.keep, got[0])
        else:
            self.value = join(self.keep, got[0], self.odd, step[1] - 2)


def arrive(sums, *others):
    gots, others = lax.optimization_barrier(([one.got for one in sums], others))
    for one, got in zip(sums, gots):
        one.got = got
        one.receive()
    return others


def doc_positions(marks):
    step_index = jnp.arange(marks.shape[-1], dtype=jnp.int32)
    starts_here = jnp.concatenate([jnp.ones((1,), bool), marks[1:] != marks[:-1]], axis=-1)
    begins = lax.cummax(jnp.where(starts_here, step_index, 0), axis=0)
    return step_index - begins


def row_table(positions, marks):
    half_index = jnp.arange(HEAD_DIM // 2, dtype=F32)
    inverse = jnp.exp(half_index * (-2.0 / HEAD_DIM) * math.log(ROPE_BASE))
    angles = positions.astype(F32)[:, None] * inverse[None, :]
    mark = jnp.broadcast_to(marks.astype(F32)[:, None], (marks.shape[0], HEAD_DIM))
    return jnp.concatenate([jnp.cos(angles), jnp.sin(angles), mark], axis=-1)


def per_device(
    residual_in,
    segments,
    first_gain,
    packed_weight,
    output_weight,
    second_gain,
    expand_weight,
    reduce_weight,
    upstream,
):
    rows, width = residual_in.shape
    me = lax.axis_index("tensor")
    heads = packed_weight.shape[2] // HEAD_DIM
    units = expand_weight.shape[2]
    barrier = lax.optimization_barrier
    gain_one, gain_two = first_gain[None, :], second_gain[None, :]
    packed = packed_weight.reshape(width, -1).T
    packed = jnp.pad(packed, ((0, -packed.shape[0] % LANES), (0, 0)))
    from_core = swap(residual_in, 1)
    from_chip = swap(residual_in, 2)

    marks = segments[0]
    positions = doc_positions(marks)
    by_block = lambda row: jnp.concatenate(
        [lax.dynamic_slice_in_dim(row, (me ^ j) * rows, rows, 0) for j in range(4)]
    )
    table = row_table(by_block(positions), by_block(marks))
    blocks = [residual_in, from_core]
    near = project(blocks, packed, gain_one, table, heads, 0)
    weights = [
        jnp.concatenate([output_weight, expand_weight[:, 0].T]),
        jnp.concatenate([expand_weight[:, 1].T, reduce_weight]),
    ]
    from_chip, near, weights = barrier((from_chip, near, weights))
    blocks += [from_chip, swap(from_chip, 1)]
    far = project(blocks[2:], packed, gain_one, table, heads, 2)

    odd = lax.axis_index("dp") % 2 == 1
    got = [swap(cut(w, odd, 0)[0], 2) for w in weights]
    from_core = [swap(w, 1) for w in weights]
    *outs_far, widened_far = attend_forward(far[0], near[1:], far[1:], (0, 1))
    outs_far, near, got[0] = barrier((outs_far, near, got[0]))
    got_first = dp_swap(got[0], 1)
    mine_far = [swap(outs_far[0], 2), swap(outs_far[1], 3)]
    core_out, core_widened = attend_forward(near[0], near[1:], far[1:], (1,))
    core_out, near, got[1], upstream_sent = barrier((core_out, near, got[1], upstream))
    got_second = dp_swap(got[1], 1)
    upstream_all = [upstream, swap(upstream, 1), swap(upstream_sent, 2)]
    own_out, own_widened = attend_forward(near[0], near[1:], far[1:], (0,))
    outs_near, mine_far, got[0], got_first = barrier(([own_out, core_out], mine_far, got[0], got_first))
    chip_first = place(got[0], got_first)
    mine = [outs_near[0], swap(outs_near[1], 1), *mine_far]
    all_first = [weights[0], from_core[0], chip_first, swap(chip_first, 1)]
    middle, normed_two = call(
        middle_kernel,
        [((rows, width), F32), ((rows, width), LOW)],
        (*mine, *all_first, residual_in, gain_two),
        2 * rows * width * width,
        "middle",
        5,
    )
    normed_two, upstream_all, *got_second = barrier((normed_two, upstream_all, got[1], got_second))
    chip_second = place(*got_second)
    all_second = [weights[1], from_core[1], chip_second, swap(chip_second, 1)]
    normed_two_all = [normed_two, swap(normed_two, 1), swap(normed_two, 2)]
    residual_out, middle_slope, second_part, *slopes = call(
        feed_kernel,
        [((rows, width), F32)] * 2
        + [((1, width), F32)]
        + [((rows, heads * HEAD_DIM), LOW)] * 4
        + [((heads * HEAD_DIM, width), LOW)] * 4,
        (*all_first, *all_second, *mine, middle, normed_two, upstream, gain_two),
        2 * rows * width * (24 * units + 2 * width),
        "feed",
        18,
        (0, 1, 3, 4, 5, 6),
    )
    slopes, output_part = slopes[:4], slopes[4:]
    slopes, output_part, normed_two_all = barrier((slopes, output_part, normed_two_all))
    slopes = [slopes[0]] + [swap(slopes[j], j) for j in (1, 2, 3)]
    from_core_sums = [swap(output_part[1], 1), swap(output_part[3], 1)]
    normed_two_all.append(swap(normed_two_all[2], 1))
    upstream_all.append(swap(upstream_all[2], 1))
    output_near = add_low(output_part[0], from_core_sums[0])
    output_far = swap(add_low(output_part[2], from_core_sums[1]), 2)
    (unit_part,) = call(
        unit_sums_kernel,
        [((3 * units, width), LOW)],
        (
            *(pltpu.with_memory_space_constraint(rows_in, pltpu.HBM) for rows_in in normed_two_all + upstream_all),
            *weights,
        ),
        48 * units * width * rows,
        "unit_sums",
        20,
    )
    unit_part, output_far = barrier((unit_part, output_far))
    unit_sum = DpSum(jnp.concatenate([unit_part, add_low(output_near, output_far)]))
    unit_sum.value, slopes[:2] = barrier((unit_sum.value, slopes[:2]))
    unit_sum.send()
    dq_near, *started = attend_backward([own_widened, core_widened], near[1:], far[1:], outs_near, slopes[:2], table)
    started, slopes = arrive([unit_sum], started, slopes)
    unit_sum.send()
    dq_far, dk, dv = attend_backward(
        [widened_far], near[1:], far[1:], outs_far, slopes[2:], table, started
    )
    (dq_far,) = arrive([unit_sum], dq_far)
    unit_sum.send()
    packed_part, first_part, *packed_slopes = call(
        partial(packed_sums_kernel, heads),
        [((3 * heads * HEAD_DIM, width), LOW), ((1, width), F32)] + [((rows, packed.shape[0]), LOW)] * 4,
        (dq_near, dq_far, dk, dv, *blocks, packed, gain_one),
        8 * rows * width * packed.shape[0],
        "packed_sums",
        8,
        scratch_shapes=[pltpu.VMEM(packed.shape, F32)],
    )
    gains = jnp.concatenate([first_part, second_part])
    gains = sum([swap(gains, j) for j in (1, 2, 3)], gains)
    packed_sum = DpSum(packed_part, gains)
    packed_sum.send()
    normed_slope = call(
        normed_slope_kernel,
        [((rows, width), kind) for kind in (F32, LOW, F32, LOW)],
        (*packed_slopes, packed),
        8 * rows * width * packed.shape[0],
        "normed_slope",
        5,
    )
    normed_slope, _ = arrive([unit_sum, packed_sum], normed_slope, pause(packed_part))
    from_core = [swap(normed_slope[1], 1), swap(normed_slope[3], 1)]
    while len(unit_sum.todo) > 1:
        unit_sum.send()
        arrive([unit_sum], pause(unit_sum.value))
    unit_sum.send()
    packed_sum.send()
    from_core, _ = arrive([packed_sum], from_core, pause(unit_sum.value))
    from_chip = swap((normed_slope[2] + from_core[1].astype(F32)).astype(LOW), 2)
    while len(packed_sum.todo) > 1:
        packed_sum.send()
        arrive([packed_sum], pause(packed_sum.value))
    packed_sum.send()
    from_chip, packed_sum.got[0], _ = arrive(
        [unit_sum], from_chip, packed_sum.got[0], pause(packed_sum.value)
    )
    unit_sum = unit_sum.value.astype(F32)
    reduce_back, output_back = unit_sum[:units], unit_sum[3 * units :]
    expand_back = unit_sum[units : 3 * units].T.reshape(width, 2, units)
    normed_slope = normed_slope[0] + from_core[0].astype(F32) + from_chip.astype(F32)
    normal, scale = normal_of(residual_in.astype(F32))
    input_back = middle_slope + norm_pull(normed_slope, normal, scale, gain_one)
    input_back, reduce_back, expand_back, output_back = arrive(
        [packed_sum], input_back, reduce_back, expand_back, output_back
    )
    packed_sum, gains = packed_sum.value.astype(F32), packed_sum.gains
    return (
        residual_out,
        input_back,
        gains[0],
        packed_sum.T.reshape(width, 3, -1),
        output_back,
        gains[1],
        expand_back,
        reduce_back,
    )


def solution(mesh):
    rows = P(("dp", "tensor"), None)
    placed = (
        rows,
        P("dp", None),
        P(),
        P(None, None, "tensor"),
        P("tensor", None),
        P(),
        P(None, None, "tensor"),
        P("tensor", None),
        rows,
    )
    return jax.shard_map(
        per_device,
        mesh=mesh,
        in_specs=placed,
        out_specs=(rows, rows, P(), placed[3], placed[4], P(), placed[6], placed[7]),
        check_vma=False,
    )
```

```python
from functools import partial
import math

import jax
import jax.numpy as jnp
from jax import lax
from jax.experimental import pallas as pl
from jax.experimental.pallas import tpu as pltpu
from jax.sharding import PartitionSpec as P

HEAD_DIM = 64
LANES = 128
EPSILON = 1e-05
ROPE_BASE = 160000.0
SCALE = 0.125
MASKED = -1000000000.0
MARKS = 4
MARK_LANE = 64
LOG_LANE = 68
SUM_LANE = 64
MIB = 2**20

F32 = jnp.float32
LOW = jnp.bfloat16
NT = (((1,), (1,)), ((), ()))
TN = (((0,), (0,)), ((), ()))


def dot(left, right):
    return jnp.dot(left, right, preferred_element_type=F32)


def against(left, right):
    return lax.dot_general(left, right, NT, preferred_element_type=F32)


def outer_sum(left, right):
    return lax.dot_general(left, right, TN, preferred_element_type=F32)


def pause_kernel(value_ref, out_ref):
    out_ref[...] = jnp.zeros_like(out_ref)


def pause(value):
    return pl.pallas_call(
        pause_kernel,
        in_specs=[pl.BlockSpec(memory_space=pl.ANY)],
        out_shape=jax.ShapeDtypeStruct((8, LANES), F32),
        cost_estimate=pl.CostEstimate(flops=10**12, bytes_accessed=10**9, transcendentals=0),
        name="pause",
    )(value)


def call(kernel, out_shapes, args, flops, name, vmem, outside=(), **rest):
    shapes = [
        (pltpu.HBM if i in outside else jax.ShapeDtypeStruct)(shape, kind)
        for i, (shape, kind) in enumerate(out_shapes)
    ]
    moved = sum(math.prod(a.shape) * jnp.dtype(a.dtype).itemsize for a in list(args) + shapes)
    return pl.pallas_call(
        kernel,
        out_shape=shapes,
        compiler_params=pltpu.CompilerParams(vmem_limit_bytes=vmem * MIB),
        cost_estimate=pl.CostEstimate(flops=int(flops) // 1000, bytes_accessed=int(moved) // 1000, transcendentals=0),
        name=name,
        **rest,
    )(*args)


def lane_of(shape):
    return lax.broadcasted_iota(jnp.int32, shape, 1)


def split_three(value):
    high = value.astype(LOW)
    rest = value - high.astype(F32)
    middle = rest.astype(LOW)
    return high, middle, (rest - middle.astype(F32)).astype(LOW)


def put_three(base, first, column):
    lane = lane_of(base.shape)
    out = base.astype(F32)
    for step, part in enumerate(split_three(column)):
        out = jnp.where(lane == first + step, part.astype(F32), out)
    return out.astype(LOW)


def rope_lanes(table):
    lane = lane_of(table.shape)
    quarter = HEAD_DIM // 2
    sine = jnp.where((lane >= quarter) & (lane < HEAD_DIM), table, 0.0)
    cosine = jnp.where(lane < quarter, table, 0.0)
    cosine = cosine + pltpu.roll(cosine, quarter, 1)
    sine = sine - pltpu.roll(sine, LANES - quarter, 1)
    return cosine + pltpu.roll(cosine, HEAD_DIM, 1), sine + pltpu.roll(sine, HEAD_DIM, 1)


def head_lanes(head, heads):
    shape = (heads * HEAD_DIM, LANES)
    source = lax.broadcasted_iota(jnp.int32, shape, 0)
    lane = lane_of(shape)
    return jnp.where((lane < HEAD_DIM) & (source == lane + head * HEAD_DIM), 1.0, 0.0).astype(LOW)


def turn_lanes(rows):
    lane = lane_of(rows.shape)
    first = lane % HEAD_DIM < HEAD_DIM // 2
    return jnp.where(first, pltpu.roll(rows, LANES - HEAD_DIM // 2, 1), pltpu.roll(rows, HEAD_DIM // 2, 1))


def packed_lanes(parts):
    keep = lane_of(parts[0].shape) < HEAD_DIM
    tiles = []
    for i in range(0, len(parts), 2):
        left = parts[i].astype(F32)
        right = pltpu.roll(parts[i + 1].astype(F32), HEAD_DIM, 1) if i + 1 < len(parts) else 0.0
        tiles.append(jnp.where(keep, left, right).astype(LOW))
    return jnp.concatenate(tiles, axis=1)


def project_kernel(heads, first, *refs):
    rows_refs, (weight_ref, gain_ref, table_ref) = refs[:2], refs[2:5]
    query_ref, key_ref, value_ref = refs[5:8]
    for b, rows_ref in enumerate(rows_refs):
        rows = rows_ref.shape[0]
        here = pl.ds(b * rows, rows)
        normed = (normal_of(rows_ref[...].astype(F32))[0] * gain_ref[...]).astype(LOW)
        packed = against(normed, weight_ref[...])
        table = table_ref[pl.ds((first + b) * rows, rows), :]
        cosine, sine = rope_lanes(table)
        lane = lane_of(table.shape)
        upper = lane - MARK_LANE
        same = upper.astype(F32) == table[:, MARK_LANE : MARK_LANE + 1]
        marks = (upper >= 0) & (upper < MARKS)
        logs = (lane >= LOG_LANE) & (lane < LOG_LANE + 3)
        sums = (lane >= SUM_LANE) & (lane < SUM_LANE + 3)
        extras = (
            jnp.where(marks & jnp.logical_not(same), MASKED, 0.0),
            jnp.where((marks & same) | logs, 1.0, 0.0),
            jnp.where(sums, 1.0, 0.0),
        )
        tiles = [packed[:, i : i + LANES] for i in range(0, packed.shape[1], LANES)]
        for i in range(3 * heads):
            rows_part = tiles[i // 2]
            part, head = i // heads, i % heads
            if part < 2:
                rows_part = rows_part * cosine + turn_lanes(rows_part) * sine
            if i % 2 == 1:
                rows_part = pltpu.roll(rows_part, HEAD_DIM, 1)
            if part == 0:
                rows_part = rows_part * SCALE
            out_ref = (query_ref, key_ref, value_ref)[part]
            out_ref[head, here, :] = jnp.where(lane < HEAD_DIM, rows_part, extras[part]).astype(LOW)


def project(blocks, weight, gain, table, heads, start):
    rows, width = blocks[0].shape
    return call(
        partial(project_kernel, heads, start),
        [((heads, 2 * rows, LANES), LOW)] * 3,
        (*blocks, weight, gain, table),
        4 * rows * width * weight.shape[0],
        "project",
        6,
    )


def forward_kernel(blocks, query_ref, near_key, far_key, near_value, far_value, *refs):
    heads, half, _ = query_ref.shape
    widened_ref = refs[-1]
    outs = {block * (half // 2): ref for block, ref in zip(blocks, refs)}
    jobs = [(head, first) for first in outs for head in range(heads)]

    def scores(head, first):
        query = query_ref[head, pl.ds(first, half // 2), :]
        return query, against(query, near_key[head]), against(query, far_key[head])

    following = scores(*jobs[0])
    for i, (head, first) in enumerate(jobs):
        query, near, far = following
        if i + 1 < len(jobs):
            following = scores(*jobs[i + 1])
        top = jnp.maximum(jnp.max(near, axis=1, keepdims=True), jnp.max(far, axis=1, keepdims=True))
        out = dot(jnp.exp(near - top).astype(LOW), near_value[head])
        out = out + dot(jnp.exp(far - top).astype(LOW), far_value[head])
        sums = out[:, SUM_LANE : SUM_LANE + 1]
        place = first - min(outs)
        widened_ref[head, pl.ds(place, half // 2), :] = put_three(query, LOG_LANE, -(top + jnp.log(sums)))
        part = against((out / sums).astype(LOW), head_lanes(head, heads))
        total = part if head == 0 else total + part
        if head == heads - 1:
            outs[first][...] = total.astype(LOW)


def attend_forward(queries, near, far, blocks):
    heads, half, _ = queries.shape
    rows = half // 2
    return call(
        partial(forward_kernel, blocks),
        [((rows, heads * HEAD_DIM), LOW)] * len(blocks) + [((heads, len(blocks) * rows, LANES), LOW)],
        (queries, near[0], far[0], near[1], far[1]),
        16 * heads * half * half * HEAD_DIM * len(blocks),
        "attend_forward",
        9,
    )


def backward_kernel(heads, chunk, last, *refs):
    near_key, far_key, near_value, far_value, out_a, out_b, slope_a, slope_b, table_ref = refs[:9]
    key_start, value_start = refs[9:11] if last else (None, None)
    queries = refs[11:-3] if last else refs[9:-3]
    dq_ref, dk_ref, dv_ref = refs[-3:]
    half = near_key.shape[1]
    pick = head_lanes(pl.program_id(0), heads)
    slope = dot(jnp.concatenate([slope_a[...], slope_b[...]]), pick)
    centre = jnp.sum(slope * dot(jnp.concatenate([out_a[...], out_b[...]]), pick), axis=1, keepdims=True)
    slope = slope.astype(LOW)
    widened = put_three(slope, SUM_LANE, -centre)
    query = jnp.concatenate([ref[0] for ref in queries])
    keep = lane_of((chunk, LANES)) < HEAD_DIM
    sides = ((near_key, near_value), (far_key, far_value))
    jobs = [(side, first) for side in (0, 1) for first in range(0, half, chunk)]

    def scores(side, first):
        keys = sides[side][0][0, pl.ds(first, chunk), :]
        values = sides[side][1][0, pl.ds(first, chunk), :]
        return keys, against(keys, query), against(values, widened)

    following = scores(*jobs[0])
    total = None
    for i, (side, first) in enumerate(jobs):
        keys, chance, drift = following
        if i + 1 < len(jobs):
            following = scores(*jobs[i + 1])
        here = pl.ds(side * half + first, chunk)
        chance = jnp.exp(chance)
        score_slope = (chance * drift).astype(LOW)
        dv = dot(chance.astype(LOW), slope)
        dk = dot(score_slope, query)
        if last:
            dk = dk + key_start[0, here, :].astype(F32)
            cosine, sine = rope_lanes(table_ref[here, :])
            dk = dk * cosine - turn_lanes(dk) * sine
            dk = jnp.where(keep, dk, 0.0)
            dv = jnp.where(keep, dv + value_start[0, here, :].astype(F32), 0.0)
        dk_ref[0, here, :] = dk.astype(LOW)
        dv_ref[0, here, :] = dv.astype(LOW)
        part = outer_sum(score_slope, keys)
        total = part if total is None else total + part
    total = total * SCALE
    cosine, sine = rope_lanes(table_ref[pl.ds(half if last else 0, half), :])
    total = total * cosine - turn_lanes(total) * sine
    dq_ref[0] = jnp.where(lane_of(total.shape) < HEAD_DIM, total, 0.0).astype(LOW)


def attend_backward(widened, near, far, outs, slopes, table, started=None):
    heads, half, _ = near[0].shape
    head = pl.BlockSpec((1, half, LANES), lambda h: (h, 0, 0))
    long = pl.BlockSpec((1, 2 * half, LANES), lambda h: (h, 0, 0))
    flat = pl.BlockSpec(outs[0].shape, lambda h: (0, 0))
    args = (near[0], far[0], near[1], far[1])
    if started is None:
        args = tuple(pltpu.with_memory_space_constraint(rows, pltpu.HBM) for rows in args)
    args += (*outs, *slopes, table)
    specs = [head] * 4 + [flat] * 4 + [pl.BlockSpec((2 * half, LANES), lambda h: (0, 0))]
    last = started is not None
    if last:
        args += tuple(started)
        specs += [long] * 2
    args += tuple(widened)
    specs += [pl.BlockSpec((1, rows.shape[1], LANES), lambda h: (h, 0, 0)) for rows in widened]
    full = (heads, 2 * half, LANES)
    return call(
        partial(backward_kernel, heads, half, last),
        [((heads, half, LANES), LOW), (full, LOW), (full, LOW)],
        args,
        80 * heads * half * half * HEAD_DIM,
        "attend_backward",
        12,
        grid=(heads,),
        in_specs=specs,
        out_specs=[head, long, long],
    )


def mean_of(rows):
    return jnp.mean(rows, axis=-1, keepdims=True)


def normal_of(rows):
    center = rows - mean_of(rows)
    scale = lax.rsqrt(mean_of(center * center) + EPSILON)
    return center * scale, scale


def norm_pull(slope, normal, scale, gain):
    inner = slope * gain
    return scale * (inner - mean_of(inner) - normal * mean_of(inner * normal))


def middle_kernel(*refs):
    attended, weights, (rows_ref, gain_ref, middle_ref, normed_ref) = refs[:4], refs[4:8], refs[8:]
    middle = rows_ref[...].astype(F32)
    for attended_ref, weight_ref in zip(attended, weights):
        middle = middle + dot(attended_ref[...], weight_ref[: attended_ref.shape[1], :])
    middle_ref[...] = middle
    normed_ref[...] = (normal_of(middle)[0] * gain_ref[...]).astype(LOW)


def gelu_parts(gate):
    bell = 0.5 * (1.0 + lax.erf(gate * math.sqrt(0.5)))
    slope = bell + gate * jnp.exp(-0.5 * gate * gate) * (1.0 / math.sqrt(2.0 * math.pi))
    return gate * bell, slope


def gated(gate, up, hidden_slope):
    active, active_slope = gelu_parts(gate)
    hidden = (active * up).astype(LOW)
    return hidden, (hidden_slope * up * active_slope).astype(LOW), (hidden_slope * active).astype(LOW)


def stacked(refs):
    return jnp.concatenate([ref[...] for ref in refs])


def feed_kernel(*refs):
    first, second = refs[:4], refs[4:8]
    attended, (middle_ref, normed_ref, upstream_ref, gain_ref) = refs[8:12], refs[12:16]
    out_ref, slope_ref, gain_sum_ref = refs[16:19]
    units = second[0].shape[0] // 2
    skip = first[0].shape[0] - units
    gate_weight = jnp.concatenate([ref[skip:, :] for ref in first])
    up_weight = jnp.concatenate([ref[:units, :] for ref in second])
    reduce = jnp.concatenate([ref[units:, :] for ref in second])
    middle, normed, upstream = middle_ref[...], normed_ref[...], upstream_ref[...]
    hidden, gate_slope, up_slope = gated(
        against(normed, gate_weight), against(normed, up_weight), against(upstream, reduce)
    )
    normed_slope = dot(gate_slope, gate_weight) + dot(up_slope, up_weight)
    normal, scale = normal_of(middle)
    slope = upstream.astype(F32) + norm_pull(normed_slope, normal, scale, gain_ref[...])
    slope_ref[...] = slope
    low = slope.astype(LOW)
    for weight_ref, attended_ref, attended_slope_ref, sum_ref in zip(first, attended, refs[19:23], refs[23:]):
        attended_slope_ref[...] = against(low, weight_ref[:skip, :]).astype(LOW)
        sum_ref[...] = outer_sum(attended_ref[...], low).astype(LOW)
    gain_sum_ref[...] = jnp.sum(normed_slope * normal, axis=0, keepdims=True)
    out_ref[...] = middle + dot(hidden, reduce)


def unit_sums_kernel(*refs):
    normed, upstream, (first_ref, second_ref, out_ref) = stacked(refs[:4]), stacked(refs[4:8]), refs[8:]
    units = second_ref.shape[0] // 2
    parts = gated(
        against(first_ref[first_ref.shape[0] - units :, :], normed),
        against(second_ref[:units, :], normed),
        against(second_ref[units:, :], upstream),
    )
    for i, (part, other) in enumerate(zip(parts, (upstream, normed, normed))):
        out_ref[pl.ds(i * units, units), :] = dot(part, other).astype(LOW)


def packed_sums_kernel(heads, *refs):
    dq_a, dq_b, dk, dv, blocks, (weight_ref, gain_ref) = *refs[:4], refs[4:8], refs[8:10]
    out_ref, gain_sum_ref, slope_refs, total_ref = refs[10], refs[11], refs[12:16], refs[16]
    rows = blocks[0].shape[0]
    used = out_ref.shape[0]
    for b in range(4):
        here = pl.ds(b * rows, rows)
        dq = dq_a if b < 2 else dq_b
        parts = [dq[h, pl.ds((b % 2) * rows, rows), :] for h in range(heads)]
        parts += [ref[h, here, :] for ref in (dk, dv) for h in range(heads)]
        slope = packed_lanes(parts)
        slope_refs[b][...] = slope
        normed = (normal_of(blocks[b][...].astype(F32))[0] * gain_ref[...]).astype(LOW)
        total = outer_sum(slope, normed)
        total_ref[...] = total if b == 0 else total_ref[...] + total
    total = total_ref[:used, :]
    out_ref[...] = total.astype(LOW)
    weight = weight_ref[:used, :].astype(F32)
    gain_sum_ref[...] = jnp.sum(total * weight, axis=0, keepdims=True) / gain_ref[...]


def normed_slope_kernel(*refs):
    slopes, weight_ref, outs = refs[:4], refs[4], refs[5:]
    for slope_ref, out_ref in zip(slopes, outs):
        out_ref[...] = dot(slope_ref[...], weight_ref[...]).astype(out_ref.dtype)


def swap(value, offset):
    size = lax.axis_size("tensor")
    return lax.ppermute(value, "tensor", [(i, i ^ offset) for i in range(size)])


def dp_swap(value, offset):
    size = lax.axis_size("dp")
    return lax.ppermute(value, "dp", [(i, i ^ offset) for i in range(size)])


def place_kernel(odd_ref, mine_ref, other_ref, out_ref):
    rows = mine_ref.shape[0]
    odd = odd_ref[0]

    @pl.when(odd == 0)
    def _():
        out_ref[:rows, :] = mine_ref[...]
        out_ref[rows:, :] = other_ref[...]

    @pl.when(odd == 1)
    def _():
        out_ref[:rows, :] = other_ref[...]
        out_ref[rows:, :] = mine_ref[...]


def place(mine, other):
    rows, width = mine.shape
    odd = (lax.axis_index("dp") % 2).astype(jnp.int32).reshape(1)
    whole = pl.BlockSpec(mine.shape, lambda: (0, 0))
    (out,) = call(
        place_kernel,
        [((2 * rows, width), LOW)],
        (odd, mine, other),
        0,
        "place",
        6,
        in_specs=[pl.BlockSpec(memory_space=pltpu.SMEM), whole, whole],
    )
    return out


def add_low(left, right):
    return (left.astype(F32) + right.astype(F32)).astype(LOW)


def cut(value, odd, axis):
    half = value.shape[axis] // 2
    lower, upper = (lax.slice_in_dim(value, i * half, (i + 1) * half, axis=axis) for i in range(2))
    return jnp.where(odd, upper, lower), jnp.where(odd, lower, upper)


def join(value, got, odd, axis):
    return jnp.concatenate([jnp.where(odd, got, value), jnp.where(odd, value, got)], axis=axis)


def gain_rows(gains, columns):
    rows = jnp.concatenate(split_three(gains)).reshape(-1, columns)
    return jnp.pad(rows, ((0, -rows.shape[0] % 16), (0, 0)))


def gain_sum(gains, rows):
    parts = rows[: 3 * gains.size // rows.shape[1]].reshape((3,) + gains.shape).astype(F32)
    return gains + parts[0] + parts[1] + parts[2]


def join_four(parts, place):
    odd, high = place % 2 == 1, place // 2 == 1
    return join(join(parts[0], parts[1], odd, 0), join(parts[2], parts[3], odd, 0), high, 0)


class DpSum:
    def __init__(self, value, gains=None):
        self.value, self.gains, self.me = value, gains, lax.axis_index("dp")
        pairs = [1 << i for i in range(2, lax.axis_size("dp").bit_length() - 1)]
        pairs = [(bit, 0 if i else 1) for i, bit in enumerate(pairs)]
        self.todo = ["scatter"] + pairs + [(bit, axis + 2) for bit, axis in reversed(pairs)] + ["gather"]

    def send(self):
        step = self.todo[0]
        place = self.me % 4
        self.rides = self.gains is not None and step != "scatter" and (step == "gather" or step[1] < 2)
        if step == "scatter":
            rows = self.value.shape[0] // 4
            parts = [lax.dynamic_slice_in_dim(self.value, (place ^ j) * rows, rows, 0) for j in range(4)]
            self.keep, sent, bits = parts[0], parts[1:], (1, 2, 3)
        elif step == "gather":
            self.keep, sent, bits = self.value, [self.value] * 3, (1, 2, 3)
        else:
            bits, self.odd = step[:1], (self.me // step[0]) % 2 == 1
            self.keep, send = cut(self.value, self.odd, step[1]) if step[1] < 2 else (self.value, self.value)
            sent = [send]
        if self.rides:
            riders = gain_rows(self.gains, sent[0].shape[1])
            sent = [jnp.concatenate([part, riders]) for part in sent]
        self.got = [dp_swap(part, bit) for part, bit in zip(sent, bits)]

    def receive(self):
        step = self.todo.pop(0)
        rows = self.keep.shape[0]
        if self.rides:
            for part in self.got:
                self.gains = gain_sum(self.gains, part[rows:])
        got = [part[:rows] for part in self.got]
        if step == "scatter":
            self.value = sum([part.astype(F32) for part in got], self.keep.astype(F32)).astype(LOW)
        elif step == "gather":
            self.value = join_four([self.keep] + got, self.me % 4)
        elif step[1] < 2:
            self.value = add_low(self.keep, got[0])
        else:
            self.value = join(self.keep, got[0], self.odd, step[1] - 2)


def arrive(sums, *others):
    gots, others = lax.optimization_barrier(([one.got for one in sums], others))
    for one, got in zip(sums, gots):
        one.got = got
        one.receive()
    return others


def doc_positions(marks):
    step_index = jnp.arange(marks.shape[-1], dtype=jnp.int32)
    starts_here = jnp.concatenate([jnp.ones((1,), bool), marks[1:] != marks[:-1]], axis=-1)
    begins = lax.cummax(jnp.where(starts_here, step_index, 0), axis=0)
    return step_index - begins


def row_table(positions, marks):
    half_index = jnp.arange(HEAD_DIM // 2, dtype=F32)
    inverse = jnp.exp(half_index * (-2.0 / HEAD_DIM) * math.log(ROPE_BASE))
    angles = positions.astype(F32)[:, None] * inverse[None, :]
    mark = jnp.broadcast_to(marks.astype(F32)[:, None], (marks.shape[0], HEAD_DIM))
    return jnp.concatenate([jnp.cos(angles), jnp.sin(angles), mark], axis=-1)


def per_device(
    residual_in,
    segments,
    first_gain,
    packed_weight,
    output_weight,
    second_gain,
    expand_weight,
    reduce_weight,
    upstream,
):
    rows, width = residual_in.shape
    me = lax.axis_index("tensor")
    heads = packed_weight.shape[2] // HEAD_DIM
    units = expand_weight.shape[2]
    barrier = lax.optimization_barrier
    gain_one, gain_two = first_gain[None, :], second_gain[None, :]
    packed = packed_weight.reshape(width, -1).T
    packed = jnp.pad(packed, ((0, -packed.shape[0] % LANES), (0, 0)))
    from_core = swap(residual_in, 1)
    from_chip = swap(residual_in, 2)

    marks = segments[0]
    positions = doc_positions(marks)
    by_block = lambda row: jnp.concatenate(
        [lax.dynamic_slice_in_dim(row, (me ^ j) * rows, rows, 0) for j in range(4)]
    )
    table = row_table(by_block(positions), by_block(marks))
    blocks = [residual_in, from_core]
    near = project(blocks, packed, gain_one, table, heads, 0)
    weights = [
        jnp.concatenate([output_weight, expand_weight[:, 0].T]),
        jnp.concatenate([expand_weight[:, 1].T, reduce_weight]),
    ]
    from_chip, near, weights = barrier((from_chip, near, weights))
    blocks += [from_chip, swap(from_chip, 1)]
    far = project(blocks[2:], packed, gain_one, table, heads, 2)

    odd = lax.axis_index("dp") % 2 == 1
    got = [swap(cut(w, odd, 0)[0], 2) for w in weights]
    from_core = [swap(w, 1) for w in weights]
    *outs_far, widened_far = attend_forward(far[0], near[1:], far[1:], (0, 1))
    outs_far, near, got[0] = barrier((outs_far, near, got[0]))
    got_first = dp_swap(got[0], 1)
    mine_far = [swap(outs_far[0], 2), swap(outs_far[1], 3)]
    core_out, core_widened = attend_forward(near[0], near[1:], far[1:], (1,))
    core_out, near, got[1], upstream_sent = barrier((core_out, near, got[1], upstream))
    got_second = dp_swap(got[1], 1)
    upstream_all = [upstream, swap(upstream, 1), swap(upstream_sent, 2)]
    own_out, own_widened = attend_forward(near[0], near[1:], far[1:], (0,))
    outs_near, mine_far, got[0], got_first = barrier(([own_out, core_out], mine_far, got[0], got_first))
    chip_first = place(got[0], got_first)
    mine = [outs_near[0], swap(outs_near[1], 1), *mine_far]
    all_first = [weights[0], from_core[0], chip_first, swap(chip_first, 1)]
    middle, normed_two = call(
        middle_kernel,
        [((rows, width), F32), ((rows, width), LOW)],
        (*mine, *all_first, residual_in, gain_two),
        2 * rows * width * width,
        "middle",
        5,
    )
    normed_two, upstream_all, *got_second = barrier((normed_two, upstream_all, got[1], got_second))
    chip_second = place(*got_second)
    all_second = [weights[1], from_core[1], chip_second, swap(chip_second, 1)]
    normed_two_all = [normed_two, swap(normed_two, 1), swap(normed_two, 2)]
    residual_out, middle_slope, second_part, *slopes = call(
        feed_kernel,
        [((rows, width), F32)] * 2
        + [((1, width), F32)]
        + [((rows, heads * HEAD_DIM), LOW)] * 4
        + [((heads * HEAD_DIM, width), LOW)] * 4,
        (*all_first, *all_second, *mine, middle, normed_two, upstream, gain_two),
        2 * rows * width * (24 * units + 2 * width),
        "feed",
        18,
        (0, 1, 3, 4, 5, 6),
    )
    slopes, output_part = slopes[:4], slopes[4:]
    slopes, output_part, normed_two_all = barrier((slopes, output_part, normed_two_all))
    slopes = [slopes[0]] + [swap(slopes[j], j) for j in (1, 2, 3)]
    from_core_sums = [swap(output_part[1], 1), swap(output_part[3], 1)]
    normed_two_all.append(swap(normed_two_all[2], 1))
    upstream_all.append(swap(upstream_all[2], 1))
    output_near = add_low(output_part[0], from_core_sums[0])
    output_far = swap(add_low(output_part[2], from_core_sums[1]), 2)
    (unit_part,) = call(
        unit_sums_kernel,
        [((3 * units, width), LOW)],
        (
            *(pltpu.with_memory_space_constraint(rows_in, pltpu.HBM) for rows_in in normed_two_all + upstream_all),
            *weights,
        ),
        48 * units * width * rows,
        "unit_sums",
        20,
    )
    unit_part, output_far = barrier((unit_part, output_far))
    unit_sum = DpSum(jnp.concatenate([unit_part, add_low(output_near, output_far)]))
    unit_sum.value, slopes[:2] = barrier((unit_sum.value, slopes[:2]))
    unit_sum.send()
    dq_near, *started = attend_backward([own_widened, core_widened], near[1:], far[1:], outs_near, slopes[:2], table)
    started, slopes = arrive([unit_sum], started, slopes)
    unit_sum.send()
    dq_far, dk, dv = attend_backward(
        [widened_far], near[1:], far[1:], outs_far, slopes[2:], table, started
    )
    (dq_far,) = arrive([unit_sum], dq_far)
    unit_sum.send()
    packed_part, first_part, *packed_slopes = call(
        partial(packed_sums_kernel, heads),
        [((3 * heads * HEAD_DIM, width), LOW), ((1, width), F32)] + [((rows, packed.shape[0]), LOW)] * 4,
        (dq_near, dq_far, dk, dv, *blocks, packed, gain_one),
        8 * rows * width * packed.shape[0],
        "packed_sums",
        8,
        scratch_shapes=[pltpu.VMEM(packed.shape, F32)],
    )
    gains = jnp.concatenate([first_part, second_part])
    gains = sum([swap(gains, j) for j in (1, 2, 3)], gains)
    packed_sum = DpSum(packed_part, gains)
    packed_sum.send()
    normed_slope = call(
        normed_slope_kernel,
        [((rows, width), kind) for kind in (F32, LOW, F32, LOW)],
        (*packed_slopes, packed),
        8 * rows * width * packed.shape[0],
        "normed_slope",
        5,
    )
    normed_slope, _ = arrive([unit_sum, packed_sum], normed_slope, pause(packed_part))
    from_core = [swap(normed_slope[1], 1), swap(normed_slope[3], 1)]
    while len(unit_sum.todo) > 1:
        unit_sum.send()
        arrive([unit_sum], pause(unit_sum.value))
    unit_sum.send()
    packed_sum.send()
    from_core, _ = arrive([packed_sum], from_core, pause(unit_sum.value))
    from_chip = swap((normed_slope[2] + from_core[1].astype(F32)).astype(LOW), 2)
    while len(packed_sum.todo) > 1:
        packed_sum.send()
        arrive([packed_sum], pause(packed_sum.value))
    packed_sum.send()
    (from_chip,) = arrive([unit_sum], from_chip)
    unit_sum = unit_sum.value.astype(F32)
    reduce_back, output_back = unit_sum[:units], unit_sum[3 * units :]
    expand_back = unit_sum[units : 3 * units].T.reshape(width, 2, units)
    normed_slope = normed_slope[0] + from_core[0].astype(F32) + from_chip.astype(F32)
    normal, scale = normal_of(residual_in.astype(F32))
    input_back = middle_slope + norm_pull(normed_slope, normal, scale, gain_one)
    input_back, reduce_back, expand_back, output_back = arrive(
        [packed_sum], input_back, reduce_back, expand_back, output_back
    )
    packed_sum, gains = packed_sum.value.astype(F32), packed_sum.gains
    return (
        residual_out,
        input_back,
        gains[0],
        packed_sum.T.reshape(width, 3, -1),
        output_back,
        gains[1],
        expand_back,
        reduce_back,
    )


def solution(mesh):
    rows = P(("dp", "tensor"), None)
    placed = (
        rows,
        P("dp", None),
        P(),
        P(None, None, "tensor"),
        P("tensor", None),
        P(),
        P(None, None, "tensor"),
        P("tensor", None),
        rows,
    )
    return jax.shard_map(
        per_device,
        mesh=mesh,
        in_specs=placed,
        out_specs=(rows, rows, P(), placed[3], placed[4], P(), placed[6], placed[7]),
        check_vma=False,
    )
```

```python
from functools import partial
import math

import jax
import jax.numpy as jnp
from jax import lax
from jax.experimental import pallas as pl
from jax.experimental.pallas import tpu as pltpu
from jax.sharding import PartitionSpec as P

HEAD_DIM = 64
LANES = 128
EPSILON = 1e-05
ROPE_BASE = 160000.0
SCALE = 0.125
MASKED = -1000000000.0
MARKS = 4
MARK_LANE = 64
LOG_LANE = 68
SUM_LANE = 64
MIB = 2**20

F32 = jnp.float32
LOW = jnp.bfloat16
NT = (((1,), (1,)), ((), ()))
TN = (((0,), (0,)), ((), ()))


def dot(left, right):
    return jnp.dot(left, right, preferred_element_type=F32)


def against(left, right):
    return lax.dot_general(left, right, NT, preferred_element_type=F32)


def outer_sum(left, right):
    return lax.dot_general(left, right, TN, preferred_element_type=F32)


def pause_kernel(value_ref, out_ref):
    out_ref[...] = jnp.zeros_like(out_ref)


def pause(value):
    return pl.pallas_call(
        pause_kernel,
        in_specs=[pl.BlockSpec(memory_space=pl.ANY)],
        out_shape=jax.ShapeDtypeStruct((8, LANES), F32),
        cost_estimate=pl.CostEstimate(flops=10**12, bytes_accessed=10**9, transcendentals=0),
        name="pause",
    )(value)


def call(kernel, out_shapes, args, flops, name, vmem, outside=(), **rest):
    shapes = [
        (pltpu.HBM if i in outside else jax.ShapeDtypeStruct)(shape, kind)
        for i, (shape, kind) in enumerate(out_shapes)
    ]
    moved = sum(math.prod(a.shape) * jnp.dtype(a.dtype).itemsize for a in list(args) + shapes)
    return pl.pallas_call(
        kernel,
        out_shape=shapes,
        compiler_params=pltpu.CompilerParams(vmem_limit_bytes=vmem * MIB),
        cost_estimate=pl.CostEstimate(flops=int(flops) // 30, bytes_accessed=int(moved) // 30, transcendentals=0),
        name=name,
        **rest,
    )(*args)


def lane_of(shape):
    return lax.broadcasted_iota(jnp.int32, shape, 1)


def split_three(value):
    high = value.astype(LOW)
    rest = value - high.astype(F32)
    middle = rest.astype(LOW)
    return high, middle, (rest - middle.astype(F32)).astype(LOW)


def put_three(base, first, column):
    lane = lane_of(base.shape)
    out = base.astype(F32)
    for step, part in enumerate(split_three(column)):
        out = jnp.where(lane == first + step, part.astype(F32), out)
    return out.astype(LOW)


def rope_lanes(table):
    lane = lane_of(table.shape)
    quarter = HEAD_DIM // 2
    sine = jnp.where((lane >= quarter) & (lane < HEAD_DIM), table, 0.0)
    cosine = jnp.where(lane < quarter, table, 0.0)
    cosine = cosine + pltpu.roll(cosine, quarter, 1)
    sine = sine - pltpu.roll(sine, LANES - quarter, 1)
    return cosine + pltpu.roll(cosine, HEAD_DIM, 1), sine + pltpu.roll(sine, HEAD_DIM, 1)


def head_lanes(head, heads):
    shape = (heads * HEAD_DIM, LANES)
    source = lax.broadcasted_iota(jnp.int32, shape, 0)
    lane = lane_of(shape)
    return jnp.where((lane < HEAD_DIM) & (source == lane + head * HEAD_DIM), 1.0, 0.0).astype(LOW)


def turn_lanes(rows):
    lane = lane_of(rows.shape)
    first = lane % HEAD_DIM < HEAD_DIM // 2
    return jnp.where(first, pltpu.roll(rows, LANES - HEAD_DIM // 2, 1), pltpu.roll(rows, HEAD_DIM // 2, 1))


def packed_lanes(parts):
    keep = lane_of(parts[0].shape) < HEAD_DIM
    tiles = []
    for i in range(0, len(parts), 2):
        left = parts[i].astype(F32)
        right = pltpu.roll(parts[i + 1].astype(F32), HEAD_DIM, 1) if i + 1 < len(parts) else 0.0
        tiles.append(jnp.where(keep, left, right).astype(LOW))
    return jnp.concatenate(tiles, axis=1)


def project_kernel(heads, first, *refs):
    rows_refs, (weight_ref, gain_ref, table_ref) = refs[:2], refs[2:5]
    query_ref, key_ref, value_ref = refs[5:8]
    for b, rows_ref in enumerate(rows_refs):
        rows = rows_ref.shape[0]
        here = pl.ds(b * rows, rows)
        normed = (normal_of(rows_ref[...].astype(F32))[0] * gain_ref[...]).astype(LOW)
        packed = against(normed, weight_ref[...])
        table = table_ref[pl.ds((first + b) * rows, rows), :]
        cosine, sine = rope_lanes(table)
        lane = lane_of(table.shape)
        upper = lane - MARK_LANE
        same = upper.astype(F32) == table[:, MARK_LANE : MARK_LANE + 1]
        marks = (upper >= 0) & (upper < MARKS)
        logs = (lane >= LOG_LANE) & (lane < LOG_LANE + 3)
        sums = (lane >= SUM_LANE) & (lane < SUM_LANE + 3)
        extras = (
            jnp.where(marks & jnp.logical_not(same), MASKED, 0.0),
            jnp.where((marks & same) | logs, 1.0, 0.0),
            jnp.where(sums, 1.0, 0.0),
        )
        tiles = [packed[:, i : i + LANES] for i in range(0, packed.shape[1], LANES)]
        for i in range(3 * heads):
            rows_part = tiles[i // 2]
            part, head = i // heads, i % heads
            if part < 2:
                rows_part = rows_part * cosine + turn_lanes(rows_part) * sine
            if i % 2 == 1:
                rows_part = pltpu.roll(rows_part, HEAD_DIM, 1)
            if part == 0:
                rows_part = rows_part * SCALE
            out_ref = (query_ref, key_ref, value_ref)[part]
            out_ref[head, here, :] = jnp.where(lane < HEAD_DIM, rows_part, extras[part]).astype(LOW)


def project(blocks, weight, gain, table, heads, start):
    rows, width = blocks[0].shape
    return call(
        partial(project_kernel, heads, start),
        [((heads, 2 * rows, LANES), LOW)] * 3,
        (*blocks, weight, gain, table),
        4 * rows * width * weight.shape[0],
        "project",
        6,
    )


def forward_kernel(blocks, query_ref, near_key, far_key, near_value, far_value, *refs):
    heads, half, _ = query_ref.shape
    widened_ref = refs[-1]
    outs = {block * (half // 2): ref for block, ref in zip(blocks, refs)}
    jobs = [(head, first) for first in outs for head in range(heads)]

    def scores(head, first):
        query = query_ref[head, pl.ds(first, half // 2), :]
        return query, against(query, near_key[head]), against(query, far_key[head])

    following = scores(*jobs[0])
    for i, (head, first) in enumerate(jobs):
        query, near, far = following
        if i + 1 < len(jobs):
            following = scores(*jobs[i + 1])
        top = jnp.maximum(jnp.max(near, axis=1, keepdims=True), jnp.max(far, axis=1, keepdims=True))
        out = dot(jnp.exp(near - top).astype(LOW), near_value[head])
        out = out + dot(jnp.exp(far - top).astype(LOW), far_value[head])
        sums = out[:, SUM_LANE : SUM_LANE + 1]
        place = first - min(outs)
        widened_ref[head, pl.ds(place, half // 2), :] = put_three(query, LOG_LANE, -(top + jnp.log(sums)))
        part = against((out / sums).astype(LOW), head_lanes(head, heads))
        total = part if head == 0 else total + part
        if head == heads - 1:
            outs[first][...] = total.astype(LOW)


def attend_forward(queries, near, far, blocks):
    heads, half, _ = queries.shape
    rows = half // 2
    return call(
        partial(forward_kernel, blocks),
        [((rows, heads * HEAD_DIM), LOW)] * len(blocks) + [((heads, len(blocks) * rows, LANES), LOW)],
        (queries, near[0], far[0], near[1], far[1]),
        16 * heads * half * half * HEAD_DIM * len(blocks),
        "attend_forward",
        9,
    )


def backward_kernel(heads, chunk, last, *refs):
    near_key, far_key, near_value, far_value, out_a, out_b, slope_a, slope_b, table_ref = refs[:9]
    key_start, value_start = refs[9:11] if last else (None, None)
    queries = refs[11:-3] if last else refs[9:-3]
    dq_ref, dk_ref, dv_ref = refs[-3:]
    half = near_key.shape[1]
    pick = head_lanes(pl.program_id(0), heads)
    slope = dot(jnp.concatenate([slope_a[...], slope_b[...]]), pick)
    centre = jnp.sum(slope * dot(jnp.concatenate([out_a[...], out_b[...]]), pick), axis=1, keepdims=True)
    slope = slope.astype(LOW)
    widened = put_three(slope, SUM_LANE, -centre)
    query = jnp.concatenate([ref[0] for ref in queries])
    keep = lane_of((chunk, LANES)) < HEAD_DIM
    sides = ((near_key, near_value), (far_key, far_value))
    jobs = [(side, first) for side in (0, 1) for first in range(0, half, chunk)]

    def scores(side, first):
        keys = sides[side][0][0, pl.ds(first, chunk), :]
        values = sides[side][1][0, pl.ds(first, chunk), :]
        return keys, against(keys, query), against(values, widened)

    following = scores(*jobs[0])
    total = None
    for i, (side, first) in enumerate(jobs):
        keys, chance, drift = following
        if i + 1 < len(jobs):
            following = scores(*jobs[i + 1])
        here = pl.ds(side * half + first, chunk)
        chance = jnp.exp(chance)
        score_slope = (chance * drift).astype(LOW)
        dv = dot(chance.astype(LOW), slope)
        dk = dot(score_slope, query)
        if last:
            dk = dk + key_start[0, here, :].astype(F32)
            cosine, sine = rope_lanes(table_ref[here, :])
            dk = dk * cosine - turn_lanes(dk) * sine
            dk = jnp.where(keep, dk, 0.0)
            dv = jnp.where(keep, dv + value_start[0, here, :].astype(F32), 0.0)
        dk_ref[0, here, :] = dk.astype(LOW)
        dv_ref[0, here, :] = dv.astype(LOW)
        part = outer_sum(score_slope, keys)
        total = part if total is None else total + part
    total = total * SCALE
    cosine, sine = rope_lanes(table_ref[pl.ds(half if last else 0, half), :])
    total = total * cosine - turn_lanes(total) * sine
    dq_ref[0] = jnp.where(lane_of(total.shape) < HEAD_DIM, total, 0.0).astype(LOW)


def attend_backward(widened, near, far, outs, slopes, table, started=None):
    heads, half, _ = near[0].shape
    head = pl.BlockSpec((1, half, LANES), lambda h: (h, 0, 0))
    long = pl.BlockSpec((1, 2 * half, LANES), lambda h: (h, 0, 0))
    flat = pl.BlockSpec(outs[0].shape, lambda h: (0, 0))
    args = (near[0], far[0], near[1], far[1])
    if started is None:
        args = tuple(pltpu.with_memory_space_constraint(rows, pltpu.HBM) for rows in args)
    args += (*outs, *slopes, table)
    specs = [head] * 4 + [flat] * 4 + [pl.BlockSpec((2 * half, LANES), lambda h: (0, 0))]
    last = started is not None
    if last:
        args += tuple(started)
        specs += [long] * 2
    args += tuple(widened)
    specs += [pl.BlockSpec((1, rows.shape[1], LANES), lambda h: (h, 0, 0)) for rows in widened]
    full = (heads, 2 * half, LANES)
    return call(
        partial(backward_kernel, heads, half, last),
        [((heads, half, LANES), LOW), (full, LOW), (full, LOW)],
        args,
        80 * heads * half * half * HEAD_DIM,
        "attend_backward",
        12,
        grid=(heads,),
        in_specs=specs,
        out_specs=[head, long, long],
    )


def mean_of(rows):
    return jnp.mean(rows, axis=-1, keepdims=True)


def normal_of(rows):
    center = rows - mean_of(rows)
    scale = lax.rsqrt(mean_of(center * center) + EPSILON)
    return center * scale, scale


def norm_pull(slope, normal, scale, gain):
    inner = slope * gain
    return scale * (inner - mean_of(inner) - normal * mean_of(inner * normal))


def middle_kernel(*refs):
    attended, weights, (rows_ref, gain_ref, middle_ref, normed_ref) = refs[:4], refs[4:8], refs[8:]
    middle = rows_ref[...].astype(F32)
    for attended_ref, weight_ref in zip(attended, weights):
        middle = middle + dot(attended_ref[...], weight_ref[: attended_ref.shape[1], :])
    middle_ref[...] = middle
    normed_ref[...] = (normal_of(middle)[0] * gain_ref[...]).astype(LOW)


def gelu_parts(gate):
    bell = 0.5 * (1.0 + lax.erf(gate * math.sqrt(0.5)))
    slope = bell + gate * jnp.exp(-0.5 * gate * gate) * (1.0 / math.sqrt(2.0 * math.pi))
    return gate * bell, slope


def gated(gate, up, hidden_slope):
    active, active_slope = gelu_parts(gate)
    hidden = (active * up).astype(LOW)
    return hidden, (hidden_slope * up * active_slope).astype(LOW), (hidden_slope * active).astype(LOW)


def stacked(refs):
    return jnp.concatenate([ref[...] for ref in refs])


def feed_kernel(*refs):
    first, second = refs[:4], refs[4:8]
    attended, (middle_ref, normed_ref, upstream_ref, gain_ref) = refs[8:12], refs[12:16]
    out_ref, slope_ref, gain_sum_ref = refs[16:19]
    units = second[0].shape[0] // 2
    skip = first[0].shape[0] - units
    gate_weight = jnp.concatenate([ref[skip:, :] for ref in first])
    up_weight = jnp.concatenate([ref[:units, :] for ref in second])
    reduce = jnp.concatenate([ref[units:, :] for ref in second])
    middle, normed, upstream = middle_ref[...], normed_ref[...], upstream_ref[...]
    hidden, gate_slope, up_slope = gated(
        against(normed, gate_weight), against(normed, up_weight), against(upstream, reduce)
    )
    normed_slope = dot(gate_slope, gate_weight) + dot(up_slope, up_weight)
    normal, scale = normal_of(middle)
    slope = upstream.astype(F32) + norm_pull(normed_slope, normal, scale, gain_ref[...])
    slope_ref[...] = slope
    low = slope.astype(LOW)
    for weight_ref, attended_ref, attended_slope_ref, sum_ref in zip(first, attended, refs[19:23], refs[23:]):
        attended_slope_ref[...] = against(low, weight_ref[:skip, :]).astype(LOW)
        sum_ref[...] = outer_sum(attended_ref[...], low).astype(LOW)
    gain_sum_ref[...] = jnp.sum(normed_slope * normal, axis=0, keepdims=True)
    out_ref[...] = middle + dot(hidden, reduce)


def unit_sums_kernel(*refs):
    normed, upstream, (first_ref, second_ref, out_ref) = stacked(refs[:4]), stacked(refs[4:8]), refs[8:]
    units = second_ref.shape[0] // 2
    parts = gated(
        against(first_ref[first_ref.shape[0] - units :, :], normed),
        against(second_ref[:units, :], normed),
        against(second_ref[units:, :], upstream),
    )
    for i, (part, other) in enumerate(zip(parts, (upstream, normed, normed))):
        out_ref[pl.ds(i * units, units), :] = dot(part, other).astype(LOW)


def packed_sums_kernel(heads, *refs):
    dq_a, dq_b, dk, dv, blocks, (weight_ref, gain_ref) = *refs[:4], refs[4:8], refs[8:10]
    out_ref, gain_sum_ref, slope_refs, total_ref = refs[10], refs[11], refs[12:16], refs[16]
    rows = blocks[0].shape[0]
    used = out_ref.shape[0]
    for b in range(4):
        here = pl.ds(b * rows, rows)
        dq = dq_a if b < 2 else dq_b
        parts = [dq[h, pl.ds((b % 2) * rows, rows), :] for h in range(heads)]
        parts += [ref[h, here, :] for ref in (dk, dv) for h in range(heads)]
        slope = packed_lanes(parts)
        slope_refs[b][...] = slope
        normed = (normal_of(blocks[b][...].astype(F32))[0] * gain_ref[...]).astype(LOW)
        total = outer_sum(slope, normed)
        total_ref[...] = total if b == 0 else total_ref[...] + total
    total = total_ref[:used, :]
    out_ref[...] = total.astype(LOW)
    weight = weight_ref[:used, :].astype(F32)
    gain_sum_ref[...] = jnp.sum(total * weight, axis=0, keepdims=True) / gain_ref[...]


def normed_slope_kernel(*refs):
    slopes, weight_ref, outs = refs[:4], refs[4], refs[5:]
    for slope_ref, out_ref in zip(slopes, outs):
        out_ref[...] = dot(slope_ref[...], weight_ref[...]).astype(out_ref.dtype)


def swap(value, offset):
    size = lax.axis_size("tensor")
    return lax.ppermute(value, "tensor", [(i, i ^ offset) for i in range(size)])


def dp_swap(value, offset):
    size = lax.axis_size("dp")
    return lax.ppermute(value, "dp", [(i, i ^ offset) for i in range(size)])


def place_kernel(odd_ref, mine_ref, other_ref, out_ref):
    rows = mine_ref.shape[0]
    odd = odd_ref[0]

    @pl.when(odd == 0)
    def _():
        out_ref[:rows, :] = mine_ref[...]
        out_ref[rows:, :] = other_ref[...]

    @pl.when(odd == 1)
    def _():
        out_ref[:rows, :] = other_ref[...]
        out_ref[rows:, :] = mine_ref[...]


def place(mine, other):
    rows, width = mine.shape
    odd = (lax.axis_index("dp") % 2).astype(jnp.int32).reshape(1)
    whole = pl.BlockSpec(mine.shape, lambda: (0, 0))
    (out,) = call(
        place_kernel,
        [((2 * rows, width), LOW)],
        (odd, mine, other),
        0,
        "place",
        6,
        in_specs=[pl.BlockSpec(memory_space=pltpu.SMEM), whole, whole],
    )
    return out


def add_low(left, right):
    return (left.astype(F32) + right.astype(F32)).astype(LOW)


def cut(value, odd, axis):
    half = value.shape[axis] // 2
    lower, upper = (lax.slice_in_dim(value, i * half, (i + 1) * half, axis=axis) for i in range(2))
    return jnp.where(odd, upper, lower), jnp.where(odd, lower, upper)


def join(value, got, odd, axis):
    return jnp.concatenate([jnp.where(odd, got, value), jnp.where(odd, value, got)], axis=axis)


def gain_rows(gains, columns):
    rows = jnp.concatenate(split_three(gains)).reshape(-1, columns)
    return jnp.pad(rows, ((0, -rows.shape[0] % 16), (0, 0)))


def gain_sum(gains, rows):
    parts = rows[: 3 * gains.size // rows.shape[1]].reshape((3,) + gains.shape).astype(F32)
    return gains + parts[0] + parts[1] + parts[2]


def join_four(parts, place):
    odd, high = place % 2 == 1, place // 2 == 1
    return join(join(parts[0], parts[1], odd, 0), join(parts[2], parts[3], odd, 0), high, 0)


class DpSum:
    def __init__(self, value, gains=None):
        self.value, self.gains, self.me = value, gains, lax.axis_index("dp")
        pairs = [1 << i for i in range(2, lax.axis_size("dp").bit_length() - 1)]
        pairs = [(bit, 0 if i else 1) for i, bit in enumerate(pairs)]
        self.todo = ["scatter"] + pairs + [(bit, axis + 2) for bit, axis in reversed(pairs)] + ["gather"]

    def send(self):
        step = self.todo[0]
        place = self.me % 4
        self.rides = self.gains is not None and step != "scatter" and (step == "gather" or step[1] < 2)
        if step == "scatter":
            rows = self.value.shape[0] // 4
            parts = [lax.dynamic_slice_in_dim(self.value, (place ^ j) * rows, rows, 0) for j in range(4)]
            self.keep, sent, bits = parts[0], parts[1:], (1, 2, 3)
        elif step == "gather":
            self.keep, sent, bits = self.value, [self.value] * 3, (1, 2, 3)
        else:
            bits, self.odd = step[:1], (self.me // step[0]) % 2 == 1
            self.keep, send = cut(self.value, self.odd, step[1]) if step[1] < 2 else (self.value, self.value)
            sent = [send]
        if self.rides:
            riders = gain_rows(self.gains, sent[0].shape[1])
            sent = [jnp.concatenate([part, riders]) for part in sent]
        self.got = [dp_swap(part, bit) for part, bit in zip(sent, bits)]

    def receive(self):
        step = self.todo.pop(0)
        rows = self.keep.shape[0]
        if self.rides:
            for part in self.got:
                self.gains = gain_sum(self.gains, part[rows:])
        got = [part[:rows] for part in self.got]
        if step == "scatter":
            self.value = sum([part.astype(F32) for part in got], self.keep.astype(F32)).astype(LOW)
        elif step == "gather":
            self.value = join_four([self.keep] + got, self.me % 4)
        elif step[1] < 2:
            self.value = add_low(self.keep, got[0])
        else:
            self.value = join(self.keep, got[0], self.odd, step[1] - 2)


def arrive(sums, *others):
    gots, others = lax.optimization_barrier(([one.got for one in sums], others))
    for one, got in zip(sums, gots):
        one.got = got
        one.receive()
    return others


def doc_positions(marks):
    step_index = jnp.arange(marks.shape[-1], dtype=jnp.int32)
    starts_here = jnp.concatenate([jnp.ones((1,), bool), marks[1:] != marks[:-1]], axis=-1)
    begins = lax.cummax(jnp.where(starts_here, step_index, 0), axis=0)
    return step_index - begins


def row_table(positions, marks):
    half_index = jnp.arange(HEAD_DIM // 2, dtype=F32)
    inverse = jnp.exp(half_index * (-2.0 / HEAD_DIM) * math.log(ROPE_BASE))
    angles = positions.astype(F32)[:, None] * inverse[None, :]
    mark = jnp.broadcast_to(marks.astype(F32)[:, None], (marks.shape[0], HEAD_DIM))
    return jnp.concatenate([jnp.cos(angles), jnp.sin(angles), mark], axis=-1)


def per_device(
    residual_in,
    segments,
    first_gain,
    packed_weight,
    output_weight,
    second_gain,
    expand_weight,
    reduce_weight,
    upstream,
):
    rows, width = residual_in.shape
    me = lax.axis_index("tensor")
    heads = packed_weight.shape[2] // HEAD_DIM
    units = expand_weight.shape[2]
    barrier = lax.optimization_barrier
    gain_one, gain_two = first_gain[None, :], second_gain[None, :]
    packed = packed_weight.reshape(width, -1).T
    packed = jnp.pad(packed, ((0, -packed.shape[0] % LANES), (0, 0)))
    from_core = swap(residual_in, 1)
    from_chip = swap(residual_in, 2)

    marks = segments[0]
    positions = doc_positions(marks)
    by_block = lambda row: jnp.concatenate(
        [lax.dynamic_slice_in_dim(row, (me ^ j) * rows, rows, 0) for j in range(4)]
    )
    table = row_table(by_block(positions), by_block(marks))
    blocks = [residual_in, from_core]
    near = project(blocks, packed, gain_one, table, heads, 0)
    weights = [
        jnp.concatenate([output_weight, expand_weight[:, 0].T]),
        jnp.concatenate([expand_weight[:, 1].T, reduce_weight]),
    ]
    from_chip, near, weights = barrier((from_chip, near, weights))
    blocks += [from_chip, swap(from_chip, 1)]
    far = project(blocks[2:], packed, gain_one, table, heads, 2)

    odd = lax.axis_index("dp") % 2 == 1
    got = [swap(cut(w, odd, 0)[0], 2) for w in weights]
    from_core = [swap(w, 1) for w in weights]
    *outs_far, widened_far = attend_forward(far[0], near[1:], far[1:], (0, 1))
    outs_far, near, got[0] = barrier((outs_far, near, got[0]))
    got_first = dp_swap(got[0], 1)
    mine_far = [swap(outs_far[0], 2), swap(outs_far[1], 3)]
    core_out, core_widened = attend_forward(near[0], near[1:], far[1:], (1,))
    core_out, near, got[1], upstream_sent = barrier((core_out, near, got[1], upstream))
    got_second = dp_swap(got[1], 1)
    upstream_all = [upstream, swap(upstream, 1), swap(upstream_sent, 2)]
    own_out, own_widened = attend_forward(near[0], near[1:], far[1:], (0,))
    outs_near, mine_far, got[0], got_first = barrier(([own_out, core_out], mine_far, got[0], got_first))
    chip_first = place(got[0], got_first)
    mine = [outs_near[0], swap(outs_near[1], 1), *mine_far]
    all_first = [weights[0], from_core[0], chip_first, swap(chip_first, 1)]
    middle, normed_two = call(
        middle_kernel,
        [((rows, width), F32), ((rows, width), LOW)],
        (*mine, *all_first, residual_in, gain_two),
        2 * rows * width * width,
        "middle",
        5,
    )
    normed_two, upstream_all, *got_second = barrier((normed_two, upstream_all, got[1], got_second))
    chip_second = place(*got_second)
    all_second = [weights[1], from_core[1], chip_second, swap(chip_second, 1)]
    normed_two_all = [normed_two, swap(normed_two, 1), swap(normed_two, 2)]
    residual_out, middle_slope, second_part, *slopes = call(
        feed_kernel,
        [((rows, width), F32)] * 2
        + [((1, width), F32)]
        + [((rows, heads * HEAD_DIM), LOW)] * 4
        + [((heads * HEAD_DIM, width), LOW)] * 4,
        (*all_first, *all_second, *mine, middle, normed_two, upstream, gain_two),
        2 * rows * width * (24 * units + 2 * width),
        "feed",
        18,
        (0, 1, 3, 4, 5, 6),
    )
    slopes, output_part = slopes[:4], slopes[4:]
    slopes, output_part, normed_two_all = barrier((slopes, output_part, normed_two_all))
    slopes = [slopes[0]] + [swap(slopes[j], j) for j in (1, 2, 3)]
    from_core_sums = [swap(output_part[1], 1), swap(output_part[3], 1)]
    normed_two_all.append(swap(normed_two_all[2], 1))
    upstream_all.append(swap(upstream_all[2], 1))
    output_near = add_low(output_part[0], from_core_sums[0])
    output_far = swap(add_low(output_part[2], from_core_sums[1]), 2)
    (unit_part,) = call(
        unit_sums_kernel,
        [((3 * units, width), LOW)],
        (
            *(pltpu.with_memory_space_constraint(rows_in, pltpu.HBM) for rows_in in normed_two_all + upstream_all),
            *weights,
        ),
        48 * units * width * rows,
        "unit_sums",
        20,
    )
    unit_part, output_far = barrier((unit_part, output_far))
    unit_sum = DpSum(jnp.concatenate([unit_part, add_low(output_near, output_far)]))
    unit_sum.value, slopes[:2] = barrier((unit_sum.value, slopes[:2]))
    unit_sum.send()
    dq_near, *started = attend_backward([own_widened, core_widened], near[1:], far[1:], outs_near, slopes[:2], table)
    started, slopes = arrive([unit_sum], started, slopes)
    unit_sum.send()
    dq_far, dk, dv = attend_backward(
        [widened_far], near[1:], far[1:], outs_far, slopes[2:], table, started
    )
    (dq_far,) = arrive([unit_sum], dq_far)
    unit_sum.send()
    packed_part, first_part, *packed_slopes = call(
        partial(packed_sums_kernel, heads),
        [((3 * heads * HEAD_DIM, width), LOW), ((1, width), F32)] + [((rows, packed.shape[0]), LOW)] * 4,
        (dq_near, dq_far, dk, dv, *blocks, packed, gain_one),
        8 * rows * width * packed.shape[0],
        "packed_sums",
        8,
        scratch_shapes=[pltpu.VMEM(packed.shape, F32)],
    )
    gains = jnp.concatenate([first_part, second_part])
    gains = sum([swap(gains, j) for j in (1, 2, 3)], gains)
    packed_sum = DpSum(packed_part, gains)
    packed_sum.send()
    normed_slope = call(
        normed_slope_kernel,
        [((rows, width), kind) for kind in (F32, LOW, F32, LOW)],
        (*packed_slopes, packed),
        8 * rows * width * packed.shape[0],
        "normed_slope",
        5,
    )
    normed_slope, _ = arrive([unit_sum, packed_sum], normed_slope, pause(packed_part))
    from_core = [swap(normed_slope[1], 1), swap(normed_slope[3], 1)]
    while len(unit_sum.todo) > 1:
        unit_sum.send()
        arrive([unit_sum], pause(unit_sum.value))
    unit_sum.send()
    packed_sum.send()
    from_core, _ = arrive([packed_sum], from_core, pause(unit_sum.value))
    from_chip = swap((normed_slope[2] + from_core[1].astype(F32)).astype(LOW), 2)
    while len(packed_sum.todo) > 1:
        packed_sum.send()
        arrive([packed_sum], pause(packed_sum.value))
    packed_sum.send()
    (from_chip,) = arrive([unit_sum], from_chip)
    unit_sum = unit_sum.value.astype(F32)
    reduce_back, output_back = unit_sum[:units], unit_sum[3 * units :]
    expand_back = unit_sum[units : 3 * units].T.reshape(width, 2, units)
    normed_slope = normed_slope[0] + from_core[0].astype(F32) + from_chip.astype(F32)
    normal, scale = normal_of(residual_in.astype(F32))
    input_back = middle_slope + norm_pull(normed_slope, normal, scale, gain_one)
    input_back, reduce_back, expand_back, output_back = arrive(
        [packed_sum], input_back, reduce_back, expand_back, output_back
    )
    packed_sum, gains = packed_sum.value.astype(F32), packed_sum.gains
    return (
        residual_out,
        input_back,
        gains[0],
        packed_sum.T.reshape(width, 3, -1),
        output_back,
        gains[1],
        expand_back,
        reduce_back,
    )


def solution(mesh):
    rows = P(("dp", "tensor"), None)
    placed = (
        rows,
        P("dp", None),
        P(),
        P(None, None, "tensor"),
        P("tensor", None),
        P(),
        P(None, None, "tensor"),
        P("tensor", None),
        rows,
    )
    return jax.shard_map(
        per_device,
        mesh=mesh,
        in_specs=placed,
        out_specs=(rows, rows, P(), placed[3], placed[4], P(), placed[6], placed[7]),
        check_vma=False,
    )
```

```python
from functools import partial
import math

import jax
import jax.numpy as jnp
from jax import lax
from jax.experimental import pallas as pl
from jax.experimental.pallas import tpu as pltpu
from jax.sharding import PartitionSpec as P

HEAD_DIM = 64
LANES = 128
EPSILON = 1e-05
ROPE_BASE = 160000.0
SCALE = 0.125
MASKED = -1000000000.0
MARKS = 4
MARK_LANE = 64
LOG_LANE = 68
SUM_LANE = 64
MIB = 2**20

F32 = jnp.float32
LOW = jnp.bfloat16
NT = (((1,), (1,)), ((), ()))
TN = (((0,), (0,)), ((), ()))


def dot(left, right):
    return jnp.dot(left, right, preferred_element_type=F32)


def against(left, right):
    return lax.dot_general(left, right, NT, preferred_element_type=F32)


def outer_sum(left, right):
    return lax.dot_general(left, right, TN, preferred_element_type=F32)


def pause_kernel(value_ref, out_ref):
    out_ref[...] = jnp.zeros_like(out_ref)


def pause(value):
    return pl.pallas_call(
        pause_kernel,
        in_specs=[pl.BlockSpec(memory_space=pl.ANY)],
        out_shape=jax.ShapeDtypeStruct((8, LANES), F32),
        cost_estimate=pl.CostEstimate(flops=10**12, bytes_accessed=10**9, transcendentals=0),
        name="pause",
    )(value)


def call(kernel, out_shapes, args, flops, name, vmem, outside=(), **rest):
    shapes = [
        (pltpu.HBM if i in outside else jax.ShapeDtypeStruct)(shape, kind)
        for i, (shape, kind) in enumerate(out_shapes)
    ]
    moved = sum(math.prod(a.shape) * jnp.dtype(a.dtype).itemsize for a in list(args) + shapes)
    return pl.pallas_call(
        kernel,
        out_shape=shapes,
        compiler_params=pltpu.CompilerParams(vmem_limit_bytes=vmem * MIB),
        cost_estimate=pl.CostEstimate(flops=int(flops) // 30, bytes_accessed=int(moved) // 30, transcendentals=0),
        name=name,
        **rest,
    )(*args)


def lane_of(shape):
    return lax.broadcasted_iota(jnp.int32, shape, 1)


def split_three(value):
    high = value.astype(LOW)
    rest = value - high.astype(F32)
    middle = rest.astype(LOW)
    return high, middle, (rest - middle.astype(F32)).astype(LOW)


def put_three(base, first, column):
    lane = lane_of(base.shape)
    out = base.astype(F32)
    for step, part in enumerate(split_three(column)):
        out = jnp.where(lane == first + step, part.astype(F32), out)
    return out.astype(LOW)


def rope_lanes(table):
    lane = lane_of(table.shape)
    quarter = HEAD_DIM // 2
    sine = jnp.where((lane >= quarter) & (lane < HEAD_DIM), table, 0.0)
    cosine = jnp.where(lane < quarter, table, 0.0)
    cosine = cosine + pltpu.roll(cosine, quarter, 1)
    sine = sine - pltpu.roll(sine, LANES - quarter, 1)
    return cosine + pltpu.roll(cosine, HEAD_DIM, 1), sine + pltpu.roll(sine, HEAD_DIM, 1)


def head_lanes(head, heads):
    shape = (heads * HEAD_DIM, LANES)
    source = lax.broadcasted_iota(jnp.int32, shape, 0)
    lane = lane_of(shape)
    return jnp.where((lane < HEAD_DIM) & (source == lane + head * HEAD_DIM), 1.0, 0.0).astype(LOW)


def turn_lanes(rows):
    lane = lane_of(rows.shape)
    first = lane % HEAD_DIM < HEAD_DIM // 2
    return jnp.where(first, pltpu.roll(rows, LANES - HEAD_DIM // 2, 1), pltpu.roll(rows, HEAD_DIM // 2, 1))


def packed_lanes(parts):
    keep = lane_of(parts[0].shape) < HEAD_DIM
    tiles = []
    for i in range(0, len(parts), 2):
        left = parts[i].astype(F32)
        right = pltpu.roll(parts[i + 1].astype(F32), HEAD_DIM, 1) if i + 1 < len(parts) else 0.0
        tiles.append(jnp.where(keep, left, right).astype(LOW))
    return jnp.concatenate(tiles, axis=1)


def project_kernel(heads, first, *refs):
    rows_refs, (weight_ref, gain_ref, table_ref) = refs[:2], refs[2:5]
    query_ref, key_ref, value_ref = refs[5:8]
    for b, rows_ref in enumerate(rows_refs):
        rows = rows_ref.shape[0]
        here = pl.ds(b * rows, rows)
        normed = (normal_of(rows_ref[...].astype(F32))[0] * gain_ref[...]).astype(LOW)
        packed = against(normed, weight_ref[...])
        table = table_ref[pl.ds((first + b) * rows, rows), :]
        cosine, sine = rope_lanes(table)
        lane = lane_of(table.shape)
        upper = lane - MARK_LANE
        same = upper.astype(F32) == table[:, MARK_LANE : MARK_LANE + 1]
        marks = (upper >= 0) & (upper < MARKS)
        logs = (lane >= LOG_LANE) & (lane < LOG_LANE + 3)
        sums = (lane >= SUM_LANE) & (lane < SUM_LANE + 3)
        extras = (
            jnp.where(marks & jnp.logical_not(same), MASKED, 0.0),
            jnp.where((marks & same) | logs, 1.0, 0.0),
            jnp.where(sums, 1.0, 0.0),
        )
        tiles = [packed[:, i : i + LANES] for i in range(0, packed.shape[1], LANES)]
        for i in range(3 * heads):
            rows_part = tiles[i // 2]
            part, head = i // heads, i % heads
            if part < 2:
                rows_part = rows_part * cosine + turn_lanes(rows_part) * sine
            if i % 2 == 1:
                rows_part = pltpu.roll(rows_part, HEAD_DIM, 1)
            if part == 0:
                rows_part = rows_part * SCALE
            out_ref = (query_ref, key_ref, value_ref)[part]
            out_ref[head, here, :] = jnp.where(lane < HEAD_DIM, rows_part, extras[part]).astype(LOW)


def project(blocks, weight, gain, table, heads, start):
    rows, width = blocks[0].shape
    return call(
        partial(project_kernel, heads, start),
        [((heads, 2 * rows, LANES), LOW)] * 3,
        (*blocks, weight, gain, table),
        4 * rows * width * weight.shape[0],
        "project",
        6,
    )


def forward_kernel(blocks, query_ref, near_key, far_key, near_value, far_value, *refs):
    heads, half, _ = query_ref.shape
    widened_ref = refs[-1]
    outs = {block * (half // 2): ref for block, ref in zip(blocks, refs)}
    jobs = [(head, first) for first in outs for head in range(heads)]

    def scores(head, first):
        query = query_ref[head, pl.ds(first, half // 2), :]
        return query, against(query, near_key[head]), against(query, far_key[head])

    following = scores(*jobs[0])
    for i, (head, first) in enumerate(jobs):
        query, near, far = following
        if i + 1 < len(jobs):
            following = scores(*jobs[i + 1])
        top = jnp.maximum(jnp.max(near, axis=1, keepdims=True), jnp.max(far, axis=1, keepdims=True))
        out = dot(jnp.exp(near - top).astype(LOW), near_value[head])
        out = out + dot(jnp.exp(far - top).astype(LOW), far_value[head])
        sums = out[:, SUM_LANE : SUM_LANE + 1]
        place = first - min(outs)
        widened_ref[head, pl.ds(place, half // 2), :] = put_three(query, LOG_LANE, -(top + jnp.log(sums)))
        part = against((out / sums).astype(LOW), head_lanes(head, heads))
        total = part if head == 0 else total + part
        if head == heads - 1:
            outs[first][...] = total.astype(LOW)


def attend_forward(queries, near, far, blocks):
    heads, half, _ = queries.shape
    rows = half // 2
    return call(
        partial(forward_kernel, blocks),
        [((rows, heads * HEAD_DIM), LOW)] * len(blocks) + [((heads, len(blocks) * rows, LANES), LOW)],
        (queries, near[0], far[0], near[1], far[1]),
        16 * heads * half * half * HEAD_DIM * len(blocks),
        "attend_forward",
        9,
    )


def backward_kernel(heads, chunk, last, *refs):
    near_key, far_key, near_value, far_value, out_a, out_b, slope_a, slope_b, table_ref = refs[:9]
    key_start, value_start = refs[9:11] if last else (None, None)
    queries = refs[11:-3] if last else refs[9:-3]
    dq_ref, dk_ref, dv_ref = refs[-3:]
    half = near_key.shape[1]
    pick = head_lanes(pl.program_id(0), heads)
    slope = dot(jnp.concatenate([slope_a[...], slope_b[...]]), pick)
    centre = jnp.sum(slope * dot(jnp.concatenate([out_a[...], out_b[...]]), pick), axis=1, keepdims=True)
    slope = slope.astype(LOW)
    widened = put_three(slope, SUM_LANE, -centre)
    query = jnp.concatenate([ref[0] for ref in queries])
    keep = lane_of((chunk, LANES)) < HEAD_DIM
    sides = ((near_key, near_value), (far_key, far_value))
    jobs = [(side, first) for side in (0, 1) for first in range(0, half, chunk)]

    def scores(side, first):
        keys = sides[side][0][0, pl.ds(first, chunk), :]
        values = sides[side][1][0, pl.ds(first, chunk), :]
        return keys, against(keys, query), against(values, widened)

    following = scores(*jobs[0])
    total = None
    for i, (side, first) in enumerate(jobs):
        keys, chance, drift = following
        if i + 1 < len(jobs):
            following = scores(*jobs[i + 1])
        here = pl.ds(side * half + first, chunk)
        chance = jnp.exp(chance)
        score_slope = (chance * drift).astype(LOW)
        dv = dot(chance.astype(LOW), slope)
        dk = dot(score_slope, query)
        if last:
            dk = dk + key_start[0, here, :].astype(F32)
            cosine, sine = rope_lanes(table_ref[here, :])
            dk = dk * cosine - turn_lanes(dk) * sine
            dk = jnp.where(keep, dk, 0.0)
            dv = jnp.where(keep, dv + value_start[0, here, :].astype(F32), 0.0)
        dk_ref[0, here, :] = dk.astype(LOW)
        dv_ref[0, here, :] = dv.astype(LOW)
        part = outer_sum(score_slope, keys)
        total = part if total is None else total + part
    total = total * SCALE
    cosine, sine = rope_lanes(table_ref[pl.ds(half if last else 0, half), :])
    total = total * cosine - turn_lanes(total) * sine
    dq_ref[0] = jnp.where(lane_of(total.shape) < HEAD_DIM, total, 0.0).astype(LOW)


def attend_backward(widened, near, far, outs, slopes, table, started=None):
    heads, half, _ = near[0].shape
    head = pl.BlockSpec((1, half, LANES), lambda h: (h, 0, 0))
    long = pl.BlockSpec((1, 2 * half, LANES), lambda h: (h, 0, 0))
    flat = pl.BlockSpec(outs[0].shape, lambda h: (0, 0))
    args = (near[0], far[0], near[1], far[1])
    if started is None:
        args = tuple(pltpu.with_memory_space_constraint(rows, pltpu.HBM) for rows in args)
    args += (*outs, *slopes, table)
    specs = [head] * 4 + [flat] * 4 + [pl.BlockSpec((2 * half, LANES), lambda h: (0, 0))]
    last = started is not None
    if last:
        args += tuple(started)
        specs += [long] * 2
    args += tuple(widened)
    specs += [pl.BlockSpec((1, rows.shape[1], LANES), lambda h: (h, 0, 0)) for rows in widened]
    full = (heads, 2 * half, LANES)
    return call(
        partial(backward_kernel, heads, half, last),
        [((heads, half, LANES), LOW), (full, LOW), (full, LOW)],
        args,
        80 * heads * half * half * HEAD_DIM,
        "attend_backward",
        12,
        grid=(heads,),
        in_specs=specs,
        out_specs=[head, long, long],
    )


def mean_of(rows):
    return jnp.mean(rows, axis=-1, keepdims=True)


def normal_of(rows):
    center = rows - mean_of(rows)
    scale = lax.rsqrt(mean_of(center * center) + EPSILON)
    return center * scale, scale


def norm_pull(slope, normal, scale, gain):
    inner = slope * gain
    return scale * (inner - mean_of(inner) - normal * mean_of(inner * normal))


def middle_kernel(*refs):
    attended, weights, (rows_ref, gain_ref, middle_ref, normed_ref) = refs[:4], refs[4:8], refs[8:]
    middle = rows_ref[...].astype(F32)
    for attended_ref, weight_ref in zip(attended, weights):
        middle = middle + dot(attended_ref[...], weight_ref[: attended_ref.shape[1], :])
    middle_ref[...] = middle
    normed_ref[...] = (normal_of(middle)[0] * gain_ref[...]).astype(LOW)


def gelu_parts(gate):
    bell = 0.5 * (1.0 + lax.erf(gate * math.sqrt(0.5)))
    slope = bell + gate * jnp.exp(-0.5 * gate * gate) * (1.0 / math.sqrt(2.0 * math.pi))
    return gate * bell, slope


def gated(gate, up, hidden_slope):
    active, active_slope = gelu_parts(gate)
    hidden = (active * up).astype(LOW)
    return hidden, (hidden_slope * up * active_slope).astype(LOW), (hidden_slope * active).astype(LOW)


def stacked(refs):
    return jnp.concatenate([ref[...] for ref in refs])


def feed_kernel(*refs):
    first, second = refs[:4], refs[4:8]
    attended, (middle_ref, normed_ref, upstream_ref, gain_ref) = refs[8:12], refs[12:16]
    out_ref, slope_ref, gain_sum_ref = refs[16:19]
    units = second[0].shape[0] // 2
    skip = first[0].shape[0] - units
    gate_weight = jnp.concatenate([ref[skip:, :] for ref in first])
    up_weight = jnp.concatenate([ref[:units, :] for ref in second])
    reduce = jnp.concatenate([ref[units:, :] for ref in second])
    middle, normed, upstream = middle_ref[...], normed_ref[...], upstream_ref[...]
    hidden, gate_slope, up_slope = gated(
        against(normed, gate_weight), against(normed, up_weight), against(upstream, reduce)
    )
    normed_slope = dot(gate_slope, gate_weight) + dot(up_slope, up_weight)
    normal, scale = normal_of(middle)
    slope = upstream.astype(F32) + norm_pull(normed_slope, normal, scale, gain_ref[...])
    slope_ref[...] = slope
    low = slope.astype(LOW)
    for weight_ref, attended_ref, attended_slope_ref, sum_ref in zip(first, attended, refs[19:23], refs[23:]):
        attended_slope_ref[...] = against(low, weight_ref[:skip, :]).astype(LOW)
        sum_ref[...] = outer_sum(attended_ref[...], low).astype(LOW)
    gain_sum_ref[...] = jnp.sum(normed_slope * normal, axis=0, keepdims=True)
    out_ref[...] = middle + dot(hidden, reduce)


def unit_sums_kernel(*refs):
    normed, upstream, (first_ref, second_ref, out_ref) = stacked(refs[:4]), stacked(refs[4:8]), refs[8:]
    units = second_ref.shape[0] // 2
    parts = gated(
        against(first_ref[first_ref.shape[0] - units :, :], normed),
        against(second_ref[:units, :], normed),
        against(second_ref[units:, :], upstream),
    )
    for i, (part, other) in enumerate(zip(parts, (upstream, normed, normed))):
        out_ref[pl.ds(i * units, units), :] = dot(part, other).astype(LOW)


def packed_sums_kernel(heads, *refs):
    dq_a, dq_b, dk, dv, blocks, (weight_ref, gain_ref) = *refs[:4], refs[4:8], refs[8:10]
    out_ref, gain_sum_ref, slope_refs, total_ref = refs[10], refs[11], refs[12:16], refs[16]
    rows = blocks[0].shape[0]
    used = out_ref.shape[0]
    for side, dq in enumerate((dq_a, dq_b)):
        slopes, normed = [], []
        for b in (2 * side, 2 * side + 1):
            here = pl.ds(b * rows, rows)
            parts = [dq[h, pl.ds((b % 2) * rows, rows), :] for h in range(heads)]
            parts += [ref[h, here, :] for ref in (dk, dv) for h in range(heads)]
            slopes.append(packed_lanes(parts))
            slope_refs[b][...] = slopes[-1]
            normed.append((normal_of(blocks[b][...].astype(F32))[0] * gain_ref[...]).astype(LOW))
        total = outer_sum(jnp.concatenate(slopes), jnp.concatenate(normed))
        total_ref[...] = total if side == 0 else total_ref[...] + total
    total = total_ref[:used, :]
    out_ref[...] = total.astype(LOW)
    weight = weight_ref[:used, :].astype(F32)
    gain_sum_ref[...] = jnp.sum(total * weight, axis=0, keepdims=True) / gain_ref[...]


def normed_slope_kernel(*refs):
    slopes, weight_ref, outs = refs[:4], refs[4], refs[5:]
    for slope_ref, out_ref in zip(slopes, outs):
        out_ref[...] = dot(slope_ref[...], weight_ref[...]).astype(out_ref.dtype)


def swap(value, offset):
    size = lax.axis_size("tensor")
    return lax.ppermute(value, "tensor", [(i, i ^ offset) for i in range(size)])


def dp_swap(value, offset):
    size = lax.axis_size("dp")
    return lax.ppermute(value, "dp", [(i, i ^ offset) for i in range(size)])


def place_kernel(odd_ref, mine_ref, other_ref, out_ref):
    rows = mine_ref.shape[0]
    odd = odd_ref[0]

    @pl.when(odd == 0)
    def _():
        out_ref[:rows, :] = mine_ref[...]
        out_ref[rows:, :] = other_ref[...]

    @pl.when(odd == 1)
    def _():
        out_ref[:rows, :] = other_ref[...]
        out_ref[rows:, :] = mine_ref[...]


def place(mine, other):
    rows, width = mine.shape
    odd = (lax.axis_index("dp") % 2).astype(jnp.int32).reshape(1)
    whole = pl.BlockSpec(mine.shape, lambda: (0, 0))
    (out,) = call(
        place_kernel,
        [((2 * rows, width), LOW)],
        (odd, mine, other),
        0,
        "place",
        6,
        in_specs=[pl.BlockSpec(memory_space=pltpu.SMEM), whole, whole],
    )
    return out


def add_low(left, right):
    return (left.astype(F32) + right.astype(F32)).astype(LOW)


def cut(value, odd, axis):
    half = value.shape[axis] // 2
    lower, upper = (lax.slice_in_dim(value, i * half, (i + 1) * half, axis=axis) for i in range(2))
    return jnp.where(odd, upper, lower), jnp.where(odd, lower, upper)


def join(value, got, odd, axis):
    return jnp.concatenate([jnp.where(odd, got, value), jnp.where(odd, value, got)], axis=axis)


def gain_rows(gains, columns):
    rows = jnp.concatenate(split_three(gains)).reshape(-1, columns)
    return jnp.pad(rows, ((0, -rows.shape[0] % 16), (0, 0)))


def gain_sum(gains, rows):
    parts = rows[: 3 * gains.size // rows.shape[1]].reshape((3,) + gains.shape).astype(F32)
    return gains + parts[0] + parts[1] + parts[2]


def join_four(parts, place):
    odd, high = place % 2 == 1, place // 2 == 1
    return join(join(parts[0], parts[1], odd, 0), join(parts[2], parts[3], odd, 0), high, 0)


class DpSum:
    def __init__(self, value, gains=None):
        self.value, self.gains, self.me = value, gains, lax.axis_index("dp")
        pairs = [1 << i for i in range(2, lax.axis_size("dp").bit_length() - 1)]
        pairs = [(bit, 0 if i else 1) for i, bit in enumerate(pairs)]
        self.todo = ["scatter"] + pairs + [(bit, axis + 2) for bit, axis in reversed(pairs)] + ["gather"]

    def send(self):
        step = self.todo[0]
        place = self.me % 4
        self.rides = self.gains is not None and step != "scatter" and (step == "gather" or step[1] < 2)
        if step == "scatter":
            rows = self.value.shape[0] // 4
            parts = [lax.dynamic_slice_in_dim(self.value, (place ^ j) * rows, rows, 0) for j in range(4)]
            self.keep, sent, bits = parts[0], parts[1:], (1, 2, 3)
        elif step == "gather":
            self.keep, sent, bits = self.value, [self.value] * 3, (1, 2, 3)
        else:
            bits, self.odd = step[:1], (self.me // step[0]) % 2 == 1
            self.keep, send = cut(self.value, self.odd, step[1]) if step[1] < 2 else (self.value, self.value)
            sent = [send]
        if self.rides:
            riders = gain_rows(self.gains, sent[0].shape[1])
            sent = [jnp.concatenate([part, riders]) for part in sent]
        self.got = [dp_swap(part, bit) for part, bit in zip(sent, bits)]

    def receive(self):
        step = self.todo.pop(0)
        rows = self.keep.shape[0]
        if self.rides:
            for part in self.got:
                self.gains = gain_sum(self.gains, part[rows:])
        got = [part[:rows] for part in self.got]
        if step == "scatter":
            self.value = sum([part.astype(F32) for part in got], self.keep.astype(F32)).astype(LOW)
        elif step == "gather":
            self.value = join_four([self.keep] + got, self.me % 4)
        elif step[1] < 2:
            self.value = add_low(self.keep, got[0])
        else:
            self.value = join(self.keep, got[0], self.odd, step[1] - 2)


def arrive(sums, *others):
    gots, others = lax.optimization_barrier(([one.got for one in sums], others))
    for one, got in zip(sums, gots):
        one.got = got
        one.receive()
    return others


def doc_positions(marks):
    step_index = jnp.arange(marks.shape[-1], dtype=jnp.int32)
    starts_here = jnp.concatenate([jnp.ones((1,), bool), marks[1:] != marks[:-1]], axis=-1)
    begins = lax.cummax(jnp.where(starts_here, step_index, 0), axis=0)
    return step_index - begins


def row_table(positions, marks):
    half_index = jnp.arange(HEAD_DIM // 2, dtype=F32)
    inverse = jnp.exp(half_index * (-2.0 / HEAD_DIM) * math.log(ROPE_BASE))
    angles = positions.astype(F32)[:, None] * inverse[None, :]
    mark = jnp.broadcast_to(marks.astype(F32)[:, None], (marks.shape[0], HEAD_DIM))
    return jnp.concatenate([jnp.cos(angles), jnp.sin(angles), mark], axis=-1)


def per_device(
    residual_in,
    segments,
    first_gain,
    packed_weight,
    output_weight,
    second_gain,
    expand_weight,
    reduce_weight,
    upstream,
):
    rows, width = residual_in.shape
    me = lax.axis_index("tensor")
    heads = packed_weight.shape[2] // HEAD_DIM
    units = expand_weight.shape[2]
    barrier = lax.optimization_barrier
    gain_one, gain_two = first_gain[None, :], second_gain[None, :]
    packed = packed_weight.reshape(width, -1).T
    packed = jnp.pad(packed, ((0, -packed.shape[0] % LANES), (0, 0)))
    from_core = swap(residual_in, 1)
    from_chip = swap(residual_in, 2)

    marks = segments[0]
    positions = doc_positions(marks)
    by_block = lambda row: jnp.concatenate(
        [lax.dynamic_slice_in_dim(row, (me ^ j) * rows, rows, 0) for j in range(4)]
    )
    table = row_table(by_block(positions), by_block(marks))
    blocks = [residual_in, from_core]
    near = project(blocks, packed, gain_one, table, heads, 0)
    weights = [
        jnp.concatenate([output_weight, expand_weight[:, 0].T]),
        jnp.concatenate([expand_weight[:, 1].T, reduce_weight]),
    ]
    from_chip, near, weights = barrier((from_chip, near, weights))
    blocks += [from_chip, swap(from_chip, 1)]
    far = project(blocks[2:], packed, gain_one, table, heads, 2)

    odd = lax.axis_index("dp") % 2 == 1
    got = [swap(cut(w, odd, 0)[0], 2) for w in weights]
    from_core = [swap(w, 1) for w in weights]
    *outs_far, widened_far = attend_forward(far[0], near[1:], far[1:], (0, 1))
    outs_far, near, got[0] = barrier((outs_far, near, got[0]))
    got_first = dp_swap(got[0], 1)
    mine_far = [swap(outs_far[0], 2), swap(outs_far[1], 3)]
    core_out, core_widened = attend_forward(near[0], near[1:], far[1:], (1,))
    core_out, near, got[1], upstream_sent = barrier((core_out, near, got[1], upstream))
    got_second = dp_swap(got[1], 1)
    upstream_all = [upstream, swap(upstream, 1), swap(upstream_sent, 2)]
    own_out, own_widened = attend_forward(near[0], near[1:], far[1:], (0,))
    outs_near, mine_far, got[0], got_first = barrier(([own_out, core_out], mine_far, got[0], got_first))
    chip_first = place(got[0], got_first)
    mine = [outs_near[0], swap(outs_near[1], 1), *mine_far]
    all_first = [weights[0], from_core[0], chip_first, swap(chip_first, 1)]
    middle, normed_two = call(
        middle_kernel,
        [((rows, width), F32), ((rows, width), LOW)],
        (*mine, *all_first, residual_in, gain_two),
        2 * rows * width * width,
        "middle",
        5,
    )
    normed_two, upstream_all, *got_second = barrier((normed_two, upstream_all, got[1], got_second))
    chip_second = place(*got_second)
    all_second = [weights[1], from_core[1], chip_second, swap(chip_second, 1)]
    normed_two_all = [normed_two, swap(normed_two, 1), swap(normed_two, 2)]
    residual_out, middle_slope, second_part, *slopes = call(
        feed_kernel,
        [((rows, width), F32)] * 2
        + [((1, width), F32)]
        + [((rows, heads * HEAD_DIM), LOW)] * 4
        + [((heads * HEAD_DIM, width), LOW)] * 4,
        (*all_first, *all_second, *mine, middle, normed_two, upstream, gain_two),
        2 * rows * width * (24 * units + 2 * width),
        "feed",
        18,
        (0, 1, 3, 4, 5, 6),
    )
    slopes, output_part = slopes[:4], slopes[4:]
    slopes, output_part, normed_two_all = barrier((slopes, output_part, normed_two_all))
    slopes = [slopes[0]] + [swap(slopes[j], j) for j in (1, 2, 3)]
    from_core_sums = [swap(output_part[1], 1), swap(output_part[3], 1)]
    normed_two_all.append(swap(normed_two_all[2], 1))
    upstream_all.append(swap(upstream_all[2], 1))
    output_near = add_low(output_part[0], from_core_sums[0])
    output_far = swap(add_low(output_part[2], from_core_sums[1]), 2)
    (unit_part,) = call(
        unit_sums_kernel,
        [((3 * units, width), LOW)],
        (
            *(pltpu.with_memory_space_constraint(rows_in, pltpu.HBM) for rows_in in normed_two_all + upstream_all),
            *weights,
        ),
        48 * units * width * rows,
        "unit_sums",
        20,
    )
    unit_part, output_far = barrier((unit_part, output_far))
    unit_sum = DpSum(jnp.concatenate([unit_part, add_low(output_near, output_far)]))
    unit_sum.value, slopes[:2] = barrier((unit_sum.value, slopes[:2]))
    unit_sum.send()
    dq_near, *started = attend_backward([own_widened, core_widened], near[1:], far[1:], outs_near, slopes[:2], table)
    started, slopes = arrive([unit_sum], started, slopes)
    unit_sum.send()
    dq_far, dk, dv = attend_backward(
        [widened_far], near[1:], far[1:], outs_far, slopes[2:], table, started
    )
    (dq_far,) = arrive([unit_sum], dq_far)
    unit_sum.send()
    packed_part, first_part, *packed_slopes = call(
        partial(packed_sums_kernel, heads),
        [((3 * heads * HEAD_DIM, width), LOW), ((1, width), F32)] + [((rows, packed.shape[0]), LOW)] * 4,
        (dq_near, dq_far, dk, dv, *blocks, packed, gain_one),
        8 * rows * width * packed.shape[0],
        "packed_sums",
        10,
        scratch_shapes=[pltpu.VMEM(packed.shape, F32)],
    )
    gains = jnp.concatenate([first_part, second_part])
    gains = sum([swap(gains, j) for j in (1, 2, 3)], gains)
    packed_sum = DpSum(packed_part, gains)
    packed_sum.send()
    normed_slope = call(
        normed_slope_kernel,
        [((rows, width), kind) for kind in (F32, LOW, F32, LOW)],
        (*packed_slopes, packed),
        8 * rows * width * packed.shape[0],
        "normed_slope",
        5,
    )
    normed_slope, _ = arrive([unit_sum, packed_sum], normed_slope, pause(packed_part))
    from_core = [swap(normed_slope[1], 1), swap(normed_slope[3], 1)]
    while len(unit_sum.todo) > 1:
        unit_sum.send()
        arrive([unit_sum], pause(unit_sum.value))
    unit_sum.send()
    packed_sum.send()
    from_core, _ = arrive([packed_sum], from_core, pause(unit_sum.value))
    from_chip = swap((normed_slope[2] + from_core[1].astype(F32)).astype(LOW), 2)
    while len(packed_sum.todo) > 1:
        packed_sum.send()
        arrive([packed_sum], pause(packed_sum.value))
    packed_sum.send()
    (from_chip,) = arrive([unit_sum], from_chip)
    unit_sum = unit_sum.value.astype(F32)
    reduce_back, output_back = unit_sum[:units], unit_sum[3 * units :]
    expand_back = unit_sum[units : 3 * units].T.reshape(width, 2, units)
    normed_slope = normed_slope[0] + from_core[0].astype(F32) + from_chip.astype(F32)
    normal, scale = normal_of(residual_in.astype(F32))
    input_back = middle_slope + norm_pull(normed_slope, normal, scale, gain_one)
    input_back, reduce_back, expand_back, output_back = arrive(
        [packed_sum], input_back, reduce_back, expand_back, output_back
    )
    packed_sum, gains = packed_sum.value.astype(F32), packed_sum.gains
    return (
        residual_out,
        input_back,
        gains[0],
        packed_sum.T.reshape(width, 3, -1),
        output_back,
        gains[1],
        expand_back,
        reduce_back,
    )


def solution(mesh):
    rows = P(("dp", "tensor"), None)
    placed = (
        rows,
        P("dp", None),
        P(),
        P(None, None, "tensor"),
        P("tensor", None),
        P(),
        P(None, None, "tensor"),
        P("tensor", None),
        rows,
    )
    return jax.shard_map(
        per_device,
        mesh=mesh,
        in_specs=placed,
        out_specs=(rows, rows, P(), placed[3], placed[4], P(), placed[6], placed[7]),
        check_vma=False,
    )
```
